256 devices in a mesh: ctx: 64 (over z, x, core), head: 4 (over y).
Axes of the slice: x: 4, y: 4, z: 8, core: 2. Of those that a mesh axis runs over, the one named last changes fastest.
Arguments:
- queries: bfloat16 [16384, 2560], P('ctx', 'head'), may hold values from -5 to 5
- keys: bfloat16 [16384, 512], P('ctx', 'head'), may hold values from -4.5 to 4.5
- values: bfloat16 [16384, 512], P('ctx', 'head'), may hold values from -6 to 6
- token_types: int32 [16384], P('ctx'), may hold values 0 or 1
- type_bias: float32 [20, 2, 2], P('head'), may hold values from -2 to 2
- out_weight: bfloat16 [2560, 5120], P('head'), may hold values from -0.125 to 0.125
Outputs:
- mixed: bfloat16 [16384, 5120], P('ctx', 'head')
The draws below stay inside these ranges and needn't reach their ends.
All inputs are finite; a program needn't handle non-finite values. No bound on the sum of `token_types` on one device may be relied on, other than what follows from the above.
Results may differ from the reference program's by a relative error of at most 0.013.
Values may be sent and summed in bfloat16 or wider, within the bound.
No kernel may reach another device: no remote copies, remote signals or barrier semaphores. Data moves between devices by JAX's collectives and lax.ppermute only.
A program may use at most 128 MiB of HBM per device.

```python
import math
import jax
import jax.numpy as jnp
from jax import lax

D = 5120
HEAD_WIDTH_SIZE = 128
GROUP = 5
HQ = 20
KEY_VALUE_HEADS = 4
TOKEN_COUNT = 16384
N_HEAD = 4


def draw_queries(key, part):
    key = jax.random.fold_in(key, 11)
    attention_output = jnp.clip(jax.random.normal(key, (TOKEN_COUNT, HQ * HEAD_WIDTH_SIZE), jnp.float32), -4.5, 4.5)
    return attention_output.astype(jnp.bfloat16)


def draw_keys(key, part):
    key = jax.random.fold_in(key, 23)
    attention_output = jnp.clip(jax.random.normal(key, (TOKEN_COUNT, KEY_VALUE_HEADS * HEAD_WIDTH_SIZE), jnp.float32), -4.5, 4.5)
    return attention_output.astype(jnp.bfloat16)


def touch_ends(drawn, stream_key, smallest, largest):
    longest = drawn.shape.index(max(drawn.shape))
    spots = []
    for shift in (0, 1):
        where = [jax.random.randint(jax.random.fold_in(stream_key, axis), (), 0, length) for axis, length in enumerate(drawn.shape)]
        where[longest] = (where[longest] + shift) % drawn.shape[longest]
        spots.append(tuple(where))
    return drawn.at[spots[0]].set(smallest).at[spots[1]].set(largest)


def level_of(own_key, extent, pieces, smallest, high):
    factor_of = 1.0
    for dim, parts in pieces:
        heights = jax.random.uniform(jax.random.fold_in(jax.random.fold_in(own_key, 6), dim), (parts,), jnp.float32, smallest / len(pieces), high / len(pieces))
        factor_of = factor_of * jnp.repeat(jnp.exp(heights), extent[dim] // parts).reshape((-1,) + (1,) * (len(extent) - 1 - dim))
    return factor_of


def gaussian(rng, dims, width, reach, cuts=(), kind=jnp.bfloat16):
    result = jax.random.normal(rng, dims, jnp.float32) * width
    if len(cuts) > 0:
        result = level_of(rng, dims, cuts, -0.22, 0.18) * result
    return jnp.clip(result, min=-reach, max=reach).astype(kind)


def setup_inputs(seed: int = 0) -> dict:
    key_of = jax.random.split(jax.random.key(seed), 7)
    return {
        "queries": draw_queries(jax.random.fold_in(key_of[6], 71), 0),
        "keys": draw_keys(jax.random.fold_in(key_of[6], 71), 0),
        "values": gaussian(key_of[2], (TOKEN_COUNT, KEY_VALUE_HEADS * HEAD_WIDTH_SIZE), 1.0, 6.0, ((0, 64), (1, 4))),
        "token_types": touch_ends((jax.random.randint(key_of[3], (TOKEN_COUNT,), 0, 2) < 1).astype(jnp.int32), jax.random.fold_in(key_of[3], 1), 0, 1),
        "type_bias": jnp.clip(jax.random.uniform(key_of[4], (HQ, 2, 2), jnp.float32, -2.0, 2.0) * level_of(key_of[4], (HQ, 2, 2), ((0, 4),), -0.4, 0.0), -2.0, 2.0),
        "out_weight": gaussian(key_of[5], (HQ * HEAD_WIDTH_SIZE, D), (HQ * HEAD_WIDTH_SIZE) ** -0.5, 0.125, ((0, 4),)),
    }


def type_term(bias_block, query_kind, key_kind):
    base_term = bias_block[:, 0, 0]
    query_step = bias_block[:, 1, 0] - bias_block[:, 0, 0]
    key_step = bias_block[:, 0, 1] - bias_block[:, 0, 0]
    joint_step = bias_block[:, 1, 1] - bias_block[:, 1, 0] - bias_block[:, 0, 1] + bias_block[:, 0, 0]
    outer_kind = query_kind[:, None] * key_kind[None, :]
    return base_term[:, None, None] + query_step[:, None, None] * query_kind[None, :, None] + key_step[:, None, None] * key_kind[None, None, :] + joint_step[:, None, None] * outer_kind[None]

def reference(queries, keys, values, token_types, type_bias, out_weight):
    seq_length = queries.shape[0]
    block_rows = math.gcd(seq_length, 512)
    score_scale = 1.0 / math.sqrt(HEAD_WIDTH_SIZE)
    positions = jnp.arange(seq_length, dtype=jnp.int32)
    kinds = token_types.astype(jnp.float32)
    total_out = jnp.zeros((seq_length, out_weight.shape[1]), jnp.float32)
    for kv_index in range(N_HEAD):
        key_block = keys[:, kv_index * HEAD_WIDTH_SIZE:(kv_index + 1) * HEAD_WIDTH_SIZE].astype(jnp.float32)
        value_block = values[:, kv_index * HEAD_WIDTH_SIZE:(kv_index + 1) * HEAD_WIDTH_SIZE].astype(jnp.float32)
        query_cols = queries[:, kv_index * GROUP * HEAD_WIDTH_SIZE:(kv_index + 1) * GROUP * HEAD_WIDTH_SIZE]
        bias_block = type_bias[kv_index * GROUP:(kv_index + 1) * GROUP].astype(jnp.float32)

        def one_block(start, query_cols=query_cols, key_block=key_block, value_block=value_block, bias_block=bias_block):
            query_rows = lax.dynamic_slice_in_dim(query_cols, start, block_rows, 0).astype(jnp.float32)
            query_rows = query_rows.reshape(block_rows, GROUP, HEAD_WIDTH_SIZE)
            query_kind = lax.dynamic_slice_in_dim(kinds, start, block_rows, 0)
            query_pos = start + jnp.arange(block_rows, dtype=jnp.int32)
            scores = jnp.einsum('qgd,kd->gqk', query_rows, key_block) * score_scale
            scores = scores + type_term(bias_block, query_kind, kinds)
            visible = positions[None, :] <= query_pos[:, None]
            scores = jnp.where(visible[None], scores, -1e+30)
            highest = lax.optimization_barrier(jnp.max(scores, axis=-1, keepdims=True))
            weights = jnp.where(visible[None], jnp.exp(scores - highest), 0.0)
            totals = lax.optimization_barrier(jnp.sum(weights, axis=-1, keepdims=True))
            rounded = lax.optimization_barrier(weights.astype(jnp.bfloat16)).astype(jnp.float32)
            summed = jnp.einsum('gqk,kd->gqd', rounded, value_block) / totals
            return jnp.transpose(summed, (1, 0, 2)).reshape(block_rows, GROUP * HEAD_WIDTH_SIZE)
        starts = jnp.arange(0, seq_length, block_rows, dtype=jnp.int32)
        blocks = lax.map(one_block, starts)
        group_attended = blocks.reshape(seq_length, GROUP * HEAD_WIDTH_SIZE).astype(jnp.bfloat16)
        weight_rows = out_weight[kv_index * GROUP * HEAD_WIDTH_SIZE:(kv_index + 1) * GROUP * HEAD_WIDTH_SIZE]
        partial_value = jnp.dot(group_attended, weight_rows, preferred_element_type=jnp.float32)
        partial_value = lax.optimization_barrier(partial_value.astype(jnp.bfloat16)).astype(jnp.float32)
        total_out = total_out + partial_value
    return total_out.astype(jnp.bfloat16)
```

```python
import functools
import math

import jax
import jax.numpy as jnp
from jax import lax
from jax.experimental import pallas as pl
from jax.experimental.pallas import tpu as pltpu
from jax.sharding import Mesh, PartitionSpec as P

f32 = jnp.float32
bf16 = jnp.bfloat16
HEAD = 128
EXTRA = 16
SUM_ROWS = 8
ACC_ROWS = HEAD + SUM_ROWS
STATE_ROWS = ACC_ROWS + 8
MASKED = -1e30
ROOM = 64.0
VMEM_LIMIT = 14 * 2**20
SMALL_LIMIT = 8 * 2**20
LOG2_SCALE = 1.4426950408889634 / math.sqrt(HEAD)


def stage_keys(blocks, first, keys_ref, values_ref):
    block = blocks[0].shape[0] - EXTRA
    row = lax.broadcasted_iota(jnp.int32, (EXTRA, HEAD), 0)
    col = lax.broadcasted_iota(jnp.int32, (EXTRA, HEAD), 1)
    spread = jnp.where((row < 2) & (col < 6) & (col % 2 == row), 1.0, 0.0).astype(bf16)
    for number, msg in enumerate(blocks):
        at = first + number * block
        keys_ref[at : at + block, :HEAD] = msg[:block, :HEAD]
        marks = lax.dot_general(
            msg[block:, :], spread, (((0,), (0,)), ((), ())), preferred_element_type=f32
        )
        keys_ref[at : at + block, HEAD:] = marks.astype(bf16)
        for part in range(block // HEAD):
            rows = slice(part * HEAD, (part + 1) * HEAD)
            cols = slice(at + part * HEAD, at + (part + 1) * HEAD)
            values_ref[:HEAD, cols] = msg[rows, HEAD:]
    total = len(blocks) * block
    values_ref[HEAD:, first : first + total] = jnp.ones((SUM_ROWS, total), bf16)


def blocks_of(refs):
    blocks = []
    for ref in refs:
        blocks += [ref] if len(ref.shape) == 2 else [ref.at[i] for i in range(ref.shape[0])]
    return blocks


def score(keys, queries):
    return lax.dot_general(keys, queries, (((1,), (1,)), ((), ())), preferred_element_type=f32)


def prepare_keys_kernel(keys_ref, values_ref, kind_ref, out_ref):
    block = keys_ref.shape[0]
    out_ref[:block, :HEAD] = keys_ref[...]
    for at in range(0, block, HEAD):
        turned = values_ref[at : at + HEAD, :].astype(f32).T
        out_ref[at : at + HEAD, HEAD:] = turned.astype(bf16)
    out_ref[block:, :] = type_marks(kind_ref)


def type_marks(kind_ref):
    kinds = jnp.broadcast_to(kind_ref[...].astype(f32), (EXTRA, kind_ref.shape[1]))
    row = lax.broadcasted_iota(jnp.int32, kinds.shape, 0)
    return jnp.where(row == 0, 1.0 - kinds, jnp.where(row == 1, kinds, 0.0)).astype(bf16)


def prepare_queries_kernel(bias_ref, query_ref, kind_ref, gate_ref, out_ref, token_ref):
    token_ref[0] = 0
    marks = type_marks(kind_ref)
    row = lax.broadcasted_iota(jnp.int32, (EXTRA, HEAD), 0)
    col = lax.broadcasted_iota(jnp.int32, (EXTRA, HEAD), 1)
    for head in range(out_ref.shape[0]):
        out_ref[head, :, :HEAD] = query_ref[:, head * HEAD : (head + 1) * HEAD]
        pairs = [bias_ref[4 * head + i] * math.sqrt(HEAD) for i in range(4)]
        first = jnp.where(col % 2 == 0, pairs[0], pairs[1])
        second = jnp.where(col % 2 == 0, pairs[2], pairs[3])
        table = jnp.where(row == 0, first, jnp.where(row == 1, second, 0.0))
        high = table.astype(bf16)
        rest = table - high.astype(f32)
        middle = rest.astype(bf16)
        low = (rest - middle.astype(f32)).astype(bf16)
        group = col // 2
        terms = jnp.where(
            group == 0,
            high.astype(f32),
            jnp.where(group == 1, middle.astype(f32), jnp.where(group == 2, low.astype(f32), 0.0)),
        ).astype(bf16)
        spread = lax.dot_general(
            marks, terms, (((0,), (0,)), ((), ())), preferred_element_type=f32
        )
        out_ref[head, :, HEAD:] = spread.astype(bf16)


def own_kernel(msgs, where_ref, mine_ref, other_ref, *refs):
    state_ref, token_ref, keys_ref, values_ref = refs[msgs:]
    blocks = blocks_of(refs[:msgs])
    slots = len(blocks)
    heads, block, _ = mine_ref.shape
    lanes = 2 * block
    stage_keys(blocks, 0, keys_ref, values_ref)
    token_ref[0] = where_ref[0] * 0
    lane = lax.broadcasted_iota(jnp.int32, (block, lanes), 1)
    query_pos = jnp.where(lane < block, where_ref[0] + lane, where_ref[1] + lane - block)
    ahead = lax.broadcasted_iota(jnp.int32, (block, lanes), 0) - query_pos

    def one_head(head, carry):
        queries = jnp.concatenate([mine_ref[head], other_ref[head]], axis=0)
        at = pl.ds(pl.multiple_of(head * lanes, HEAD), lanes)
        peak = jnp.full((1, lanes), MASKED, f32)
        parts = []
        for slot in range(slots):
            piece = score(keys_ref[slot * block : (slot + 1) * block, :], queries)
            piece = jnp.where(ahead <= -where_ref[2 + slot], piece, MASKED)
            peak = jnp.maximum(peak, jnp.max(piece, axis=0, keepdims=True))
            parts.append(piece)
        peak = jnp.where(peak > 0.5 * MASKED, peak, 0.0)
        shift = peak * LOG2_SCALE
        weights = jnp.concatenate(
            [jnp.exp2(part * LOG2_SCALE - shift).astype(bf16) for part in parts], axis=0
        )
        state_ref[:ACC_ROWS, at] = jnp.dot(values_ref[...], weights, preferred_element_type=f32)
        state_ref[ACC_ROWS:, at] = jnp.broadcast_to(peak, (8, lanes))
        return carry

    lax.fori_loop(0, heads, one_head, 0)


def add_keys(count, mine_ref, other_ref, keys_ref, values_ref, size, old_ref, state_ref):
    heads, block, _ = mine_ref.shape
    lanes = 2 * block
    state_ref[...] = old_ref[...]

    def queries_of(head):
        return jnp.concatenate([mine_ref[head], other_ref[head]], axis=0)

    def lanes_of(head):
        return pl.ds(pl.multiple_of(head * lanes, HEAD), lanes)

    def unit(step, worst):
        head, plane = step % heads, step // heads
        at = lanes_of(head)
        part = pl.ds(pl.multiple_of(plane * size, size), size)
        peak = old_ref[ACC_ROWS : ACC_ROWS + 1, at]
        mass = old_ref[HEAD : HEAD + 1, at]
        scores = score(keys_ref[part, :], queries_of(head))
        top = jnp.max(scores, axis=0, keepdims=True)
        weights = jnp.exp2(scores * LOG2_SCALE - peak * LOG2_SCALE).astype(bf16)
        state_ref[:ACC_ROWS, at] += jnp.dot(
            values_ref[:, part], weights, preferred_element_type=f32
        )
        rise = (top - peak) * LOG2_SCALE
        bad = (rise > ROOM) | ((mass <= 0.0) & (rise < -ROOM))
        return jnp.maximum(worst, jnp.where(bad, 1.0, 0.0))

    worst = lax.fori_loop(0, count, lambda p, w: functools.reduce(lambda w, h: unit(p * heads + h, w), range(heads), w), jnp.zeros((1, lanes), f32))

    @pl.when(jnp.max(worst) > 0.5)
    def _():
        state_ref[...] = old_ref[...]
        step_rows = 256
        chunks = size // step_rows

        def redo(step, carry):
            at = lanes_of(step % heads)
            part = pl.ds(pl.multiple_of((step // heads) * step_rows, step_rows), step_rows)
            peak = state_ref[ACC_ROWS : ACC_ROWS + 1, at]
            mass = state_ref[HEAD : HEAD + 1, at]
            scores = score(keys_ref[part, :], queries_of(step % heads))
            top = jnp.max(scores, axis=0, keepdims=True)
            fresh = jnp.where(mass > 0.0, jnp.maximum(peak, top), top)
            fade = jnp.where(mass > 0.0, jnp.exp2((peak - fresh) * LOG2_SCALE), 0.0)
            weights = jnp.exp2(scores * LOG2_SCALE - fresh * LOG2_SCALE).astype(bf16)
            update = jnp.dot(values_ref[:, part], weights, preferred_element_type=f32)
            state_ref[:ACC_ROWS, at] = state_ref[:ACC_ROWS, at] * fade + update
            state_ref[ACC_ROWS:, at] = jnp.broadcast_to(fresh, (8, lanes))
            return carry

        lax.fori_loop(0, heads * count * chunks, redo, 0)


def plane_kernel(plan, last, gates, count_ref, mine_ref, other_ref, *refs):
    msgs = 1 + max(index for plane in plan for index, _ in plane)
    old_ref = refs[msgs]
    if last:
        kept_ref, parcel_ref, state_ref, keys_ref, values_ref = refs[msgs + 1 + gates :]
    else:
        state_ref, token_ref, keys_ref, values_ref = refs[msgs + 1 + gates :]
    blocks = [blocks_of([ref]) for ref in refs[:msgs]]
    heads, block, _ = mine_ref.shape
    size = len(plan[0]) * block
    count = count_ref[0]
    for number, plane in enumerate(plan):

        @pl.when(count > number)
        def _(number=number, plane=plane):
            stage_keys([blocks[i][j] for i, j in plane], number * size, keys_ref, values_ref)

    add_keys(count, mine_ref, other_ref, keys_ref, values_ref, size, old_ref, state_ref)
    if not last:
        token_ref[0] = count * 0
        return
    for head in range(heads):
        finish(block, head, state_ref, kept_ref.at[head], parcel_ref.at[head])


def finish(block, head, state_ref, kept_ref, parcel_ref):
    at = slice(head * 2 * block, (head + 1) * 2 * block)
    mass = state_ref[HEAD : HEAD + 1, at]
    peak = state_ref[ACC_ROWS : ACC_ROWS + 1, at]
    full = mass > 0.0
    safe = jnp.where(full, mass, 1.0)
    level = jnp.where(full, peak * LOG2_SCALE + jnp.log2(safe), MASKED)
    mean = state_ref[:HEAD, at] * (1.0 / safe)
    kept_ref[:HEAD, :] = mean[:, :block]
    kept_ref[HEAD:, :] = jnp.broadcast_to(level[:, :block], (8, block))
    parcel_ref[:HEAD, :] = mean[:, block:].astype(bf16)
    whole = jnp.broadcast_to(level[:, block:], (EXTRA, block))
    high = whole.astype(bf16)
    rest = whole - high.astype(f32)
    middle = rest.astype(bf16)
    low = rest - middle.astype(f32)
    row = lax.broadcasted_iota(jnp.int32, whole.shape, 0)
    parcel_ref[HEAD:, :] = jnp.where(
        row == 0,
        high.astype(f32),
        jnp.where(row == 1, middle.astype(f32), jnp.where(row == 2, low, 0.0)),
    ).astype(bf16)


def merge_kernel(kept_ref, came_ref, low_ref, high_ref):
    half = low_ref.shape[0]
    for head in range(kept_ref.shape[0]):
        kept_level = kept_ref[head, HEAD : HEAD + 1, :]
        extra = came_ref[head, HEAD:, :].astype(f32)
        came_level = extra[0:1] + extra[1:2] + extra[2:3]
        top = jnp.maximum(kept_level, came_level)
        kept_part = jnp.exp2(kept_level - top)
        came_part = jnp.exp2(came_level - top)
        share = 1.0 / (kept_part + came_part)
        mixed = kept_ref[head, :HEAD, :] * (kept_part * share) + came_ref[head, :HEAD, :].astype(
            f32
        ) * (came_part * share)
        cols = slice(head * HEAD, (head + 1) * HEAD)
        low_ref[:, cols] = mixed[:, :half].T.astype(bf16)
        high_ref[:, cols] = mixed[:, half:].T.astype(bf16)


def tick_kernel(*refs):
    refs[-1][0] = 0


def after(*values):
    return pl.pallas_call(
        tick_kernel,
        in_specs=[pl.BlockSpec(memory_space=pl.ANY)] * len(values),
        out_specs=IN_SMEM,
        out_shape=jax.ShapeDtypeStruct((1,), jnp.int32),
        name="after",
    )(*values)[0]


def whole(value):
    return pl.BlockSpec(value.shape, lambda *_: (0,) * value.ndim)


IN_VMEM = pl.BlockSpec(memory_space=pltpu.VMEM)
IN_SMEM = pl.BlockSpec(memory_space=pltpu.SMEM)


def attend_own(where, mine, other, msgs):
    heads, block, depth = mine.shape
    lanes = 2 * block
    total = block * sum(1 if m.ndim == 2 else m.shape[0] for m in msgs)
    return pl.pallas_call(
        functools.partial(own_kernel, len(msgs)),
        in_specs=[IN_SMEM] + [IN_VMEM] * (2 + len(msgs)),
        out_specs=[IN_VMEM, IN_SMEM],
        scratch_shapes=[pltpu.VMEM((total, 2 * HEAD), bf16), pltpu.VMEM((ACC_ROWS, total), bf16)],
        out_shape=[
            jax.ShapeDtypeStruct((STATE_ROWS, heads * lanes), f32),
            jax.ShapeDtypeStruct((1,), jnp.int32),
        ],
        compiler_params=pltpu.CompilerParams(vmem_limit_bytes=VMEM_LIMIT),
        cost_estimate=pl.CostEstimate(
            flops=8 * heads * lanes * total * 256, bytes_accessed=2**20, transcendentals=0
        ),
        name="own_plane",
    )(where, mine, other, *msgs)


def attend_planes(count, mine, other, msgs, plan, state, last=False, gates=()):
    heads, block, depth = mine.shape
    lanes = 2 * block
    total = block * sum(len(plane) for plane in plan)
    scratch = [pltpu.VMEM((total, 2 * HEAD), bf16), pltpu.VMEM((ACC_ROWS, total), bf16)]
    if last:
        out_specs = [IN_VMEM, IN_VMEM]
        out_shape = [
            jax.ShapeDtypeStruct((heads, ACC_ROWS, block), f32),
            jax.ShapeDtypeStruct((heads, STATE_ROWS, block), bf16),
        ]
        scratch = [pltpu.VMEM((STATE_ROWS, heads * lanes), f32)] + scratch
    else:
        out_specs = [IN_VMEM, IN_SMEM]
        out_shape = [
            jax.ShapeDtypeStruct((STATE_ROWS, heads * lanes), f32),
            jax.ShapeDtypeStruct((1,), jnp.int32),
        ]
    return pl.pallas_call(
        functools.partial(plane_kernel, plan, last, len(gates)),
        in_specs=[IN_SMEM]
        + [IN_VMEM] * (3 + len(msgs))
        + [pl.BlockSpec(memory_space=pl.ANY)] * len(gates),
        out_specs=out_specs,
        scratch_shapes=scratch,
        out_shape=out_shape,
        compiler_params=pltpu.CompilerParams(vmem_limit_bytes=VMEM_LIMIT),
        cost_estimate=pl.CostEstimate(
            flops=6 * heads * lanes * total * 256, bytes_accessed=2**20, transcendentals=0
        ),
        name="last_planes" if last else "planes",
    )(count, mine, other, *msgs, state, *gates)


def joined(pair):
    return jnp.concatenate([pair[0][...], pair[1][...]], axis=0)


def near_kernel(core_ref, own, below, above, weights, out_ref):
    own_w, got_w, their_w = weights
    rows, width = below[0].shape[1], got_w.shape[1]
    out_ref[...] = jnp.dot(joined(own), own_w[...], preferred_element_type=f32)
    sides = jnp.concatenate([joined(below), joined(above)], axis=1)
    for side, weight in enumerate((got_w, their_w)):
        place = jnp.where(core_ref[0] == side, 0, width)
        at = pl.ds(pl.multiple_of(place, HEAD), width)
        out_ref[:, at] += jnp.dot(sides, weight[: 2 * rows, :], preferred_element_type=f32)


def far_kernel(core_ref, near_ref, pair, weights, out_ref):
    part = joined(pair)
    rows, width = part.shape[1], weights[0].shape[1]
    for side, weight in enumerate(weights):
        place = jnp.where(core_ref[0] == side, 0, width)
        at = pl.ds(pl.multiple_of(place, HEAD), width)
        more = jnp.dot(part, weight[2 * rows :, :], preferred_element_type=f32)
        out_ref[:, at] = (near_ref[:, at] + more).astype(bf16)


def project_near(core, own, below, above, weights):
    block, cols = 2 * own[0].shape[0], weights[0].shape[1]
    return pl.pallas_call(
        near_kernel,
        in_specs=[IN_SMEM, [IN_VMEM] * 2, [IN_VMEM] * 2, [IN_VMEM] * 2, [IN_VMEM] * 3],
        out_specs=IN_VMEM,
        out_shape=jax.ShapeDtypeStruct((block, cols), f32),
        compiler_params=pltpu.CompilerParams(vmem_limit_bytes=VMEM_LIMIT),
        name="project_near",
    )(core, list(own), below, above, weights)


def project_far(core, near, pair, weights):
    return pl.pallas_call(
        far_kernel,
        in_specs=[IN_SMEM, IN_VMEM, [IN_VMEM] * 2, [IN_VMEM] * 2],
        out_specs=IN_VMEM,
        out_shape=jax.ShapeDtypeStruct(near.shape, bf16),
        compiler_params=pltpu.CompilerParams(vmem_limit_bytes=VMEM_LIMIT),
        name="project_far",
    )(core, near, pair, weights)


def shift(value, axis, size, step):
    return lax.ppermute(value, axis, [(i, (i + step) % size) for i in range(size)])


def shards(sizes, queries, keys, values, token_types, type_bias, out_weight):
    nz, nx, nc, ny = sizes
    zi, xi, ci, yi = (lax.axis_index(a) for a in ("z", "x", "core", "head"))
    block = queries.shape[0]
    heads = type_bias.shape[0]
    kinds = token_types.reshape(1, block)

    message = pl.pallas_call(
        prepare_keys_kernel,
        out_shape=jax.ShapeDtypeStruct((block + EXTRA, 2 * HEAD), bf16),
        name="prepare_keys",
    )(keys, values, kinds)

    across = shift(message, "x", nx, 2)
    right = shift(message, "x", nx, 1)
    left = shift(message, "x", nx, -1)
    mine, token = pl.pallas_call(
        prepare_queries_kernel,
        in_specs=[IN_SMEM, IN_VMEM, IN_VMEM, pl.BlockSpec(memory_space=pl.ANY)],
        out_specs=[IN_VMEM, IN_SMEM],
        out_shape=[
            jax.ShapeDtypeStruct((heads, block, 2 * HEAD), bf16),
            jax.ShapeDtypeStruct((1,), jnp.int32),
        ],
        name="prepare_queries",
    )(type_bias.reshape(-1), queries, kinds, left)
    other = shift(mine, "core", nc, 1)
    plane = jnp.stack([message, right, across, left])

    forward, backward = [plane], [plane]
    for _ in range(3):
        forward.append(shift(forward[-1], "z", nz, 1))
        backward.append(shift(backward[-1], "z", nz, -1))
    far_parts = [forward[3][: nx // 2], backward[3][nx // 2 :]]
    far = [shift(far_parts[0], "z", nz, 1), shift(far_parts[1], "z", nz, -1)]

    rows_w, cols_w = out_weight.shape[0], out_weight.shape[1] // ny
    half = cols_w // nc

    def carve(step, gate, first=ci * half, cols=half):
        col = ((yi + step) % ny) * cols_w + first
        return lax.dynamic_slice(out_weight, (gate, col), (rows_w, cols))

    far_w = shift(carve(2, token[0]), "head", ny, 2)
    gate = after(plane)
    up_w = shift(carve(1, gate), "head", ny, 1)
    down_w = shift(carve(-1, gate), "head", ny, -1)

    chip = (zi * nx + xi) * nc
    homes = [((zi * nx + (xi - d) % nx) * nc + ci) * block for d in range(nx)]
    where = jnp.stack([(chip + ci) * block, (chip + 1 - ci) * block] + homes).astype(jnp.int32)
    state, token = attend_own(where, mine, other, [plane])
    planes = tuple(tuple((i, j) for j in range(nx)) for i in range(2))
    for step in (1, 2, 3):
        count = jnp.stack([jnp.where(zi >= nz - step, 2, jnp.where(zi >= step, 1, 0))])
        state, token = attend_planes(
            count.astype(jnp.int32),
            mine,
            other,
            [forward[step], backward[step]],
            planes,
            state,
            gates=far_parts if step == 3 else (),
        )
    got_w = jnp.concatenate([up_w, down_w, far_w]) + token[0].astype(bf16)
    their_w = shift(got_w, "core", nc, 1)
    own_w = carve(0, token[0], 0, cols_w)
    count = jnp.stack([jnp.where(zi >= nz // 2, 1, 0)]).astype(jnp.int32)
    kept, parcel = attend_planes(
        count, mine, other, far, (((0, 0), (0, 1), (1, 0), (1, 1)),), state, last=True
    )

    came = shift(parcel, "core", nc, 1)
    own = pl.pallas_call(
        merge_kernel,
        out_shape=[jax.ShapeDtypeStruct((block // 2, heads * HEAD), bf16)] * 2,
        compiler_params=pltpu.CompilerParams(vmem_limit_bytes=SMALL_LIMIT),
        name="merge",
    )(kept, came)

    below = [shift(own[0], "head", ny, 1), None]
    above = [None, shift(own[1], "head", ny, -1)]
    below[1] = shift(own[1], "head", ny, 1)
    above[0] = shift(own[0], "head", ny, -1)
    opposite = [shift(below[0], "head", ny, 1), shift(above[1], "head", ny, -1)]
    core = jnp.stack([ci]).astype(jnp.int32)
    near = project_near(core, own, below, above, [own_w, got_w, their_w])
    return project_far(core, near, opposite, [got_w, their_w])


def solution(mesh):
    nz, nx, nc, ny = 8, 4, 2, 4
    grid = Mesh(mesh.devices.reshape(nz, nx, nc, ny), ("z", "x", "core", "head"))
    ctx = ("z", "x", "core")
    in_specs = (
        P(ctx, "head"),
        P(ctx, "head"),
        P(ctx, "head"),
        P(ctx),
        P("head", None, None),
        P("head", None),
    )
    return jax.shard_map(
        functools.partial(shards, (nz, nx, nc, ny)),
        mesh=grid,
        in_specs=in_specs,
        out_specs=P(ctx, "head"),
        check_vma=False,
    )
```

```python
import functools
import math

import jax
import jax.numpy as jnp
from jax import lax
from jax.experimental import pallas as pl
from jax.experimental.pallas import tpu as pltpu
from jax.sharding import Mesh, PartitionSpec as P

f32 = jnp.float32
bf16 = jnp.bfloat16
HEAD = 128
EXTRA = 16
SUM_ROWS = 8
ACC_ROWS = HEAD + SUM_ROWS
STATE_ROWS = ACC_ROWS + 8
MASKED = -1e30
ROOM = 64.0
VMEM_LIMIT = 12 * 2**20
SMALL_LIMIT = 8 * 2**20
LOG2_SCALE = 1.4426950408889634 / math.sqrt(HEAD)


def stage_keys(blocks, first, keys_ref, values_ref):
    block = blocks[0].shape[0] - EXTRA
    row = lax.broadcasted_iota(jnp.int32, (EXTRA, HEAD), 0)
    col = lax.broadcasted_iota(jnp.int32, (EXTRA, HEAD), 1)
    spread = jnp.where((row < 2) & (col < 6) & (col % 2 == row), 1.0, 0.0).astype(bf16)
    for number, msg in enumerate(blocks):
        at = first + number * block
        keys_ref[at : at + block, :HEAD] = msg[:block, :HEAD]
        marks = lax.dot_general(
            msg[block:, :], spread, (((0,), (0,)), ((), ())), preferred_element_type=f32
        )
        keys_ref[at : at + block, HEAD:] = marks.astype(bf16)
        for part in range(block // HEAD):
            rows = slice(part * HEAD, (part + 1) * HEAD)
            cols = slice(at + part * HEAD, at + (part + 1) * HEAD)
            values_ref[:HEAD, cols] = msg[rows, HEAD:]
    total = len(blocks) * block
    values_ref[HEAD:, first : first + total] = jnp.ones((SUM_ROWS, total), bf16)


def blocks_of(refs):
    blocks = []
    for ref in refs:
        blocks += [ref] if len(ref.shape) == 2 else [ref.at[i] for i in range(ref.shape[0])]
    return blocks


def score(keys, queries):
    return lax.dot_general(keys, queries, (((1,), (1,)), ((), ())), preferred_element_type=f32)


def prepare_keys_kernel(keys_ref, values_ref, kind_ref, out_ref, token_ref):
    token_ref[0] = 0
    block = keys_ref.shape[0]
    out_ref[:block, :HEAD] = keys_ref[...]
    for at in range(0, block, HEAD):
        turned = values_ref[at : at + HEAD, :].astype(f32).T
        out_ref[at : at + HEAD, HEAD:] = turned.astype(bf16)
    out_ref[block:, :] = type_marks(kind_ref)


def type_marks(kind_ref):
    kinds = jnp.broadcast_to(kind_ref[...].astype(f32), (EXTRA, kind_ref.shape[1]))
    row = lax.broadcasted_iota(jnp.int32, kinds.shape, 0)
    return jnp.where(row == 0, 1.0 - kinds, jnp.where(row == 1, kinds, 0.0)).astype(bf16)


def prepare_queries_kernel(bias_ref, query_ref, kind_ref, gate_ref, out_ref, token_ref):
    token_ref[0] = 0
    marks = type_marks(kind_ref)
    row = lax.broadcasted_iota(jnp.int32, (EXTRA, HEAD), 0)
    col = lax.broadcasted_iota(jnp.int32, (EXTRA, HEAD), 1)
    for head in range(out_ref.shape[0]):
        out_ref[head, :, :HEAD] = query_ref[:, head * HEAD : (head + 1) * HEAD]
        pairs = [bias_ref[4 * head + i] * math.sqrt(HEAD) for i in range(4)]
        first = jnp.where(col % 2 == 0, pairs[0], pairs[1])
        second = jnp.where(col % 2 == 0, pairs[2], pairs[3])
        table = jnp.where(row == 0, first, jnp.where(row == 1, second, 0.0))
        high = table.astype(bf16)
        rest = table - high.astype(f32)
        middle = rest.astype(bf16)
        low = (rest - middle.astype(f32)).astype(bf16)
        group = col // 2
        terms = jnp.where(
            group == 0,
            high.astype(f32),
            jnp.where(group == 1, middle.astype(f32), jnp.where(group == 2, low.astype(f32), 0.0)),
        ).astype(bf16)
        spread = lax.dot_general(
            marks, terms, (((0,), (0,)), ((), ())), preferred_element_type=f32
        )
        out_ref[head, :, HEAD:] = spread.astype(bf16)


def own_kernel(msgs, where_ref, mine_ref, other_ref, *refs):
    state_ref, token_ref, keys_ref, values_ref = refs[msgs:]
    blocks = blocks_of(refs[:msgs])
    slots = len(blocks)
    heads, block, _ = mine_ref.shape
    lanes = 2 * block
    stage_keys(blocks, 0, keys_ref, values_ref)
    token_ref[0] = where_ref[0] * 0
    lane = lax.broadcasted_iota(jnp.int32, (block, lanes), 1)
    query_pos = jnp.where(lane < block, where_ref[0] + lane, where_ref[1] + lane - block)
    ahead = lax.broadcasted_iota(jnp.int32, (block, lanes), 0) - query_pos

    def one_head(head, carry):
        queries = jnp.concatenate([mine_ref[head], other_ref[head]], axis=0)
        at = pl.ds(pl.multiple_of(head * lanes, HEAD), lanes)
        peak = jnp.full((1, lanes), MASKED, f32)
        parts = []
        for slot in range(slots):
            piece = score(keys_ref[slot * block : (slot + 1) * block, :], queries)
            piece = jnp.where(ahead <= -where_ref[2 + slot], piece, MASKED)
            peak = jnp.maximum(peak, jnp.max(piece, axis=0, keepdims=True))
            parts.append(piece)
        peak = jnp.where(peak > 0.5 * MASKED, peak, 0.0)
        shift = peak * LOG2_SCALE
        weights = jnp.concatenate(
            [jnp.exp2(part * LOG2_SCALE - shift).astype(bf16) for part in parts], axis=0
        )
        state_ref[:ACC_ROWS, at] = jnp.dot(values_ref[...], weights, preferred_element_type=f32)
        state_ref[ACC_ROWS:, at] = jnp.broadcast_to(peak, (8, lanes))
        return carry

    lax.fori_loop(0, heads, one_head, 0)


def add_keys(count, mine_ref, other_ref, keys_ref, values_ref, size, old_ref, state_ref):
    heads, block, _ = mine_ref.shape
    lanes = 2 * block
    state_ref[...] = old_ref[...]

    def queries_of(head):
        return jnp.concatenate([mine_ref[head], other_ref[head]], axis=0)

    def lanes_of(head):
        return pl.ds(pl.multiple_of(head * lanes, HEAD), lanes)

    def unit(step, worst):
        head, plane = step % heads, step // heads
        at = lanes_of(head)
        part = pl.ds(pl.multiple_of(plane * size, size), size)
        peak = old_ref[ACC_ROWS : ACC_ROWS + 1, at]
        mass = old_ref[HEAD : HEAD + 1, at]
        scores = score(keys_ref[part, :], queries_of(head))
        top = jnp.max(scores, axis=0, keepdims=True)
        weights = jnp.exp2(scores * LOG2_SCALE - peak * LOG2_SCALE).astype(bf16)
        state_ref[:ACC_ROWS, at] += jnp.dot(
            values_ref[:, part], weights, preferred_element_type=f32
        )
        rise = (top - peak) * LOG2_SCALE
        bad = (rise > ROOM) | ((mass <= 0.0) & (rise < -ROOM))
        return jnp.maximum(worst, jnp.where(bad, 1.0, 0.0))

    worst = lax.fori_loop(0, count, lambda p, w: functools.reduce(lambda w, h: unit(p * heads + h, w), range(heads), w), jnp.zeros((1, lanes), f32))

    @pl.when(jnp.max(worst) > 0.5)
    def _():
        state_ref[...] = old_ref[...]
        step_rows = 256
        chunks = size // step_rows

        def redo(step, carry):
            at = lanes_of(step % heads)
            part = pl.ds(pl.multiple_of((step // heads) * step_rows, step_rows), step_rows)
            peak = state_ref[ACC_ROWS : ACC_ROWS + 1, at]
            mass = state_ref[HEAD : HEAD + 1, at]
            scores = score(keys_ref[part, :], queries_of(step % heads))
            top = jnp.max(scores, axis=0, keepdims=True)
            fresh = jnp.where(mass > 0.0, jnp.maximum(peak, top), top)
            fade = jnp.where(mass > 0.0, jnp.exp2((peak - fresh) * LOG2_SCALE), 0.0)
            weights = jnp.exp2(scores * LOG2_SCALE - fresh * LOG2_SCALE).astype(bf16)
            update = jnp.dot(values_ref[:, part], weights, preferred_element_type=f32)
            state_ref[:ACC_ROWS, at] = state_ref[:ACC_ROWS, at] * fade + update
            state_ref[ACC_ROWS:, at] = jnp.broadcast_to(fresh, (8, lanes))
            return carry

        lax.fori_loop(0, heads * count * chunks, redo, 0)


def plane_kernel(plan, last, gates, count_ref, mine_ref, other_ref, *refs):
    msgs = 1 + max(index for plane in plan for index, _ in plane)
    old_ref = refs[msgs]
    if last:
        kept_ref, parcel_ref, token_ref, state_ref, keys_ref, values_ref = refs[msgs + 1 + gates :]
    else:
        state_ref, token_ref, keys_ref, values_ref = refs[msgs + 1 + gates :]
    blocks = [blocks_of([ref]) for ref in refs[:msgs]]
    heads, block, _ = mine_ref.shape
    size = len(plan[0]) * block
    count = count_ref[0]
    for number, plane in enumerate(plan):

        @pl.when(count > number)
        def _(number=number, plane=plane):
            stage_keys([blocks[i][j] for i, j in plane], number * size, keys_ref, values_ref)

    add_keys(count, mine_ref, other_ref, keys_ref, values_ref, size, old_ref, state_ref)
    token_ref[0] = count * 0
    if not last:
        return
    for head in range(heads):
        finish(block, head, state_ref, kept_ref.at[head], parcel_ref.at[head])


def finish(block, head, state_ref, kept_ref, parcel_ref):
    at = slice(head * 2 * block, (head + 1) * 2 * block)
    mass = state_ref[HEAD : HEAD + 1, at]
    peak = state_ref[ACC_ROWS : ACC_ROWS + 1, at]
    full = mass > 0.0
    safe = jnp.where(full, mass, 1.0)
    level = jnp.where(full, peak * LOG2_SCALE + jnp.log2(safe), MASKED)
    mean = state_ref[:HEAD, at] * (1.0 / safe)
    kept_ref[:HEAD, :] = mean[:, :block]
    kept_ref[HEAD:, :] = jnp.broadcast_to(level[:, :block], (8, block))
    parcel_ref[:HEAD, :] = mean[:, block:].astype(bf16)
    whole = jnp.broadcast_to(level[:, block:], (EXTRA, block))
    high = whole.astype(bf16)
    rest = whole - high.astype(f32)
    middle = rest.astype(bf16)
    low = rest - middle.astype(f32)
    row = lax.broadcasted_iota(jnp.int32, whole.shape, 0)
    parcel_ref[HEAD:, :] = jnp.where(
        row == 0,
        high.astype(f32),
        jnp.where(row == 1, middle.astype(f32), jnp.where(row == 2, low, 0.0)),
    ).astype(bf16)


def merge_kernel(kept_ref, came_ref, low_ref, high_ref, token_ref):
    token_ref[0] = 0
    half = low_ref.shape[0]
    for head in range(kept_ref.shape[0]):
        kept_level = kept_ref[head, HEAD : HEAD + 1, :]
        extra = came_ref[head, HEAD:, :].astype(f32)
        came_level = extra[0:1] + extra[1:2] + extra[2:3]
        top = jnp.maximum(kept_level, came_level)
        kept_part = jnp.exp2(kept_level - top)
        came_part = jnp.exp2(came_level - top)
        share = 1.0 / (kept_part + came_part)
        mixed = kept_ref[head, :HEAD, :] * (kept_part * share) + came_ref[head, :HEAD, :].astype(
            f32
        ) * (came_part * share)
        cols = slice(head * HEAD, (head + 1) * HEAD)
        low_ref[:, cols] = mixed[:, :half].T.astype(bf16)
        high_ref[:, cols] = mixed[:, half:].T.astype(bf16)


def whole(value):
    return pl.BlockSpec(value.shape, lambda *_: (0,) * value.ndim)


IN_VMEM = pl.BlockSpec(memory_space=pltpu.VMEM)
IN_SMEM = pl.BlockSpec(memory_space=pltpu.SMEM)


def attend_own(where, mine, other, msgs):
    heads, block, depth = mine.shape
    lanes = 2 * block
    total = block * sum(1 if m.ndim == 2 else m.shape[0] for m in msgs)
    return pl.pallas_call(
        functools.partial(own_kernel, len(msgs)),
        in_specs=[IN_SMEM] + [IN_VMEM] * (2 + len(msgs)),
        out_specs=[IN_VMEM, IN_SMEM],
        scratch_shapes=[pltpu.VMEM((total, 2 * HEAD), bf16), pltpu.VMEM((ACC_ROWS, total), bf16)],
        out_shape=[
            jax.ShapeDtypeStruct((STATE_ROWS, heads * lanes), f32),
            jax.ShapeDtypeStruct((1,), jnp.int32),
        ],
        compiler_params=pltpu.CompilerParams(vmem_limit_bytes=VMEM_LIMIT),
        cost_estimate=pl.CostEstimate(
            flops=8 * heads * lanes * total * 256, bytes_accessed=2**20, transcendentals=0
        ),
        name="own_plane",
    )(where, mine, other, *msgs)


def attend_planes(count, mine, other, msgs, plan, state, last=False, gates=()):
    heads, block, depth = mine.shape
    lanes = 2 * block
    total = block * sum(len(plane) for plane in plan)
    scratch = [pltpu.VMEM((total, 2 * HEAD), bf16), pltpu.VMEM((ACC_ROWS, total), bf16)]
    if last:
        out_specs = [IN_VMEM, IN_VMEM, IN_SMEM]
        out_shape = [
            jax.ShapeDtypeStruct((heads, ACC_ROWS, block), f32),
            jax.ShapeDtypeStruct((heads, STATE_ROWS, block), bf16),
            jax.ShapeDtypeStruct((1,), jnp.int32),
        ]
        scratch = [pltpu.VMEM((STATE_ROWS, heads * lanes), f32)] + scratch
    else:
        out_specs = [IN_VMEM, IN_SMEM]
        out_shape = [
            jax.ShapeDtypeStruct((STATE_ROWS, heads * lanes), f32),
            jax.ShapeDtypeStruct((1,), jnp.int32),
        ]
    return pl.pallas_call(
        functools.partial(plane_kernel, plan, last, len(gates)),
        in_specs=[IN_SMEM]
        + [IN_VMEM] * (3 + len(msgs))
        + [pl.BlockSpec(memory_space=pl.ANY)] * len(gates),
        out_specs=out_specs,
        scratch_shapes=scratch,
        out_shape=out_shape,
        compiler_params=pltpu.CompilerParams(vmem_limit_bytes=VMEM_LIMIT),
        cost_estimate=pl.CostEstimate(
            flops=6 * heads * lanes * total * 256, bytes_accessed=2**20, transcendentals=0
        ),
        name="last_planes" if last else "planes",
    )(count, mine, other, *msgs, state, *gates)


def joined(pair):
    return jnp.concatenate([pair[0][...], pair[1][...]], axis=0)


def near_kernel(core_ref, own, below, above, own_w, up_w, down_w, out_ref):
    rows, width = up_w[0].shape
    out_ref[...] = jnp.dot(joined(own), own_w[...], preferred_element_type=f32)
    low, high = joined(below), joined(above)
    for side in range(2):
        first = jnp.where(core_ref[0] == side, 0, width)
        at = pl.ds(pl.multiple_of(first, HEAD), width)
        more = jnp.dot(low, up_w[side][...], preferred_element_type=f32)
        out_ref[:, at] += more + jnp.dot(high, down_w[side][...], preferred_element_type=f32)


def far_kernel(core_ref, near_ref, pair, far_w, out_ref):
    part = joined(pair)
    width = far_w[0].shape[1]
    for side in range(2):
        first = jnp.where(core_ref[0] == side, 0, width)
        at = pl.ds(pl.multiple_of(first, HEAD), width)
        more = jnp.dot(part, far_w[side][...], preferred_element_type=f32)
        out_ref[:, at] = (near_ref[:, at] + more).astype(bf16)


def project_near(core, own, below, above, own_w, up_w, down_w):
    block, cols = 2 * own[0].shape[0], own_w.shape[1]
    pair = [IN_VMEM] * 2
    return pl.pallas_call(
        near_kernel,
        in_specs=[IN_SMEM, pair, pair, pair, IN_VMEM, pair, pair],
        out_specs=IN_VMEM,
        out_shape=jax.ShapeDtypeStruct((block, cols), f32),
        compiler_params=pltpu.CompilerParams(vmem_limit_bytes=VMEM_LIMIT),
        name="project_near",
    )(core, list(own), below, above, own_w, up_w, down_w)


def project_far(core, near, opposite, far_w):
    pair = [IN_VMEM] * 2
    return pl.pallas_call(
        far_kernel,
        in_specs=[IN_SMEM, IN_VMEM, pair, pair],
        out_specs=IN_VMEM,
        out_shape=jax.ShapeDtypeStruct(near.shape, bf16),
        compiler_params=pltpu.CompilerParams(vmem_limit_bytes=VMEM_LIMIT),
        name="project_far",
    )(core, near, opposite, far_w)


def carve_kernel(column_ref, weight_ref, out_ref, sem):
    column = pl.multiple_of(column_ref[0], HEAD)
    copy = pltpu.make_async_copy(weight_ref.at[:, pl.ds(column, out_ref.shape[1])], out_ref, sem)
    copy.start()
    copy.wait()


def take_columns(column, weight, width):
    rows = weight.shape[0]
    return pl.pallas_call(
        carve_kernel,
        in_specs=[IN_SMEM, pl.BlockSpec(memory_space=pltpu.HBM)],
        out_specs=IN_VMEM,
        out_shape=jax.ShapeDtypeStruct((rows, width), weight.dtype),
        scratch_shapes=[pltpu.SemaphoreType.DMA],
        compiler_params=pltpu.CompilerParams(vmem_limit_bytes=SMALL_LIMIT),
        name="carve",
    )(column, weight)


def shift(value, axis, size, step):
    return lax.ppermute(value, axis, [(i, (i + step) % size) for i in range(size)])


def with_sibling(weight, token):
    weight = weight + token[0].astype(bf16)
    return [weight, shift(weight, "core", 2, 1)]


def shards(sizes, queries, keys, values, token_types, type_bias, out_weight):
    nz, nx, nc, ny = sizes
    zi, xi, ci, yi = (lax.axis_index(a) for a in ("z", "x", "core", "head"))
    block = queries.shape[0]
    heads = type_bias.shape[0]
    kinds = token_types.reshape(1, block)

    message, early = pl.pallas_call(
        prepare_keys_kernel,
        out_specs=[IN_VMEM, IN_SMEM],
        out_shape=[
            jax.ShapeDtypeStruct((block + EXTRA, 2 * HEAD), bf16),
            jax.ShapeDtypeStruct((1,), jnp.int32),
        ],
        name="prepare_keys",
    )(keys, values, kinds)

    across = shift(message, "x", nx, 2)
    right = shift(message, "x", nx, 1)
    left = shift(message, "x", nx, -1)
    plane = jnp.stack([message, right, across, left])
    mine, ready = pl.pallas_call(
        prepare_queries_kernel,
        in_specs=[IN_SMEM] + [IN_VMEM] * 3,
        out_specs=[IN_VMEM, IN_SMEM],
        out_shape=[
            jax.ShapeDtypeStruct((heads, block, 2 * HEAD), bf16),
            jax.ShapeDtypeStruct((1,), jnp.int32),
        ],
        name="prepare_queries",
    )(type_bias.reshape(-1), queries, kinds, plane)
    other = shift(mine, "core", nc, 1)

    forward, backward = [plane], [plane]

    def onward(token):
        zero = 0 if token is None else token[0].astype(bf16)
        forward.append(shift(forward[-1] + zero, "z", nz, 1))
        backward.append(shift(backward[-1] + zero, "z", nz, -1))

    onward(None)

    rows_w, cols_w = out_weight.shape[0], out_weight.shape[1] // ny
    half = cols_w // nc

    def column(step):
        return ((yi + step) % ny) * cols_w + ci * half

    up_w, down_w = [
        shift(
            lax.dynamic_slice(out_weight, (0, column(step) + ready[0]), (rows_w, half)),
            "head",
            ny,
            step,
        )
        for step in (1, -1)
    ]

    chip = (zi * nx + xi) * nc
    homes = [((zi * nx + (xi - d) % nx) * nc + ci) * block for d in range(nx)]
    where = jnp.stack([(chip + ci) * block, (chip + 1 - ci) * block] + homes).astype(jnp.int32)
    state, token = attend_own(where, mine, other, [plane])
    far_w = shift(
        take_columns((column(2) + token).astype(jnp.int32), out_weight, half), "head", ny, 2
    )
    onward(token)
    onward(None)
    far_parts = [forward[3][: nx // 2], backward[3][nx // 2 :]]
    far = [shift(far_parts[0], "z", nz, 1), shift(far_parts[1], "z", nz, -1)]
    planes = tuple(tuple((i, j) for j in range(nx)) for i in range(2))
    for step in (1, 2, 3):
        count = jnp.stack([jnp.where(zi >= nz - step, 2, jnp.where(zi >= step, 1, 0))])
        state, token = attend_planes(
            count.astype(jnp.int32),
            mine,
            other,
            [forward[step], backward[step]],
            planes,
            state,
            gates=far_parts if step == 3 else (),
        )
        if step == 2:
            up_w, down_w = with_sibling(up_w, token), with_sibling(down_w, token)
    count = jnp.stack([jnp.where(zi >= nz // 2, 1, 0)]).astype(jnp.int32)
    kept, parcel, token = attend_planes(
        count, mine, other, far, (((0, 0), (0, 1), (1, 0), (1, 1)),), state, last=True
    )

    came = shift(parcel, "core", nc, 1)
    *own, merged = pl.pallas_call(
        merge_kernel,
        out_specs=[IN_VMEM, IN_VMEM, IN_SMEM],
        out_shape=[jax.ShapeDtypeStruct((block // 2, heads * HEAD), bf16)] * 2
        + [jax.ShapeDtypeStruct((1,), jnp.int32)],
        compiler_params=pltpu.CompilerParams(vmem_limit_bytes=SMALL_LIMIT),
        name="merge",
    )(kept, came)

    below = [shift(own[0], "head", ny, 1), None]
    above = [None, shift(own[1], "head", ny, -1)]
    below[1] = shift(own[1], "head", ny, 1)
    above[0] = shift(own[0], "head", ny, -1)
    opposite = [shift(below[0], "head", ny, 1), shift(above[1], "head", ny, -1)]
    own_w = lax.dynamic_slice(out_weight, (0, yi * cols_w + token[0]), (rows_w, cols_w))
    core = jnp.stack([ci]).astype(jnp.int32)
    near = project_near(core, own, below, above, own_w, up_w, down_w)
    return project_far(core, near, opposite, with_sibling(far_w, merged))


def solution(mesh):
    nz, nx, nc, ny = 8, 4, 2, 4
    grid = Mesh(mesh.devices.reshape(nz, nx, nc, ny), ("z", "x", "core", "head"))
    ctx = ("z", "x", "core")
    in_specs = (
        P(ctx, "head"),
        P(ctx, "head"),
        P(ctx, "head"),
        P(ctx),
        P("head", None, None),
        P("head", None),
    )
    return jax.shard_map(
        functools.partial(shards, (nz, nx, nc, ny)),
        mesh=grid,
        in_specs=in_specs,
        out_specs=P(ctx, "head"),
        check_vma=False,
    )
```

```python
import functools
import math

import jax
import jax.numpy as jnp
from jax import lax
from jax.experimental import pallas as pl
from jax.experimental.pallas import tpu as pltpu
from jax.sharding import Mesh, PartitionSpec as P

f32 = jnp.float32
bf16 = jnp.bfloat16
HEAD = 128
EXTRA = 16
SUM_ROWS = 8
ACC_ROWS = HEAD + SUM_ROWS
STATE_ROWS = ACC_ROWS + 8
MASKED = -1e30
ROOM = 64.0
VMEM_LIMIT = 12 * 2**20
SMALL_LIMIT = 8 * 2**20
LOG2_SCALE = 1.4426950408889634 / math.sqrt(HEAD)


def stage_keys(blocks, first, keys_ref, values_ref):
    block = blocks[0].shape[0] - EXTRA
    row = lax.broadcasted_iota(jnp.int32, (EXTRA, HEAD), 0)
    col = lax.broadcasted_iota(jnp.int32, (EXTRA, HEAD), 1)
    spread = jnp.where((row < 2) & (col < 6) & (col % 2 == row), 1.0, 0.0).astype(bf16)
    for number, msg in enumerate(blocks):
        at = first + number * block
        keys_ref[at : at + block, :HEAD] = msg[:block, :HEAD]
        marks = lax.dot_general(
            msg[block:, :], spread, (((0,), (0,)), ((), ())), preferred_element_type=f32
        )
        keys_ref[at : at + block, HEAD:] = marks.astype(bf16)
        for part in range(block // HEAD):
            rows = slice(part * HEAD, (part + 1) * HEAD)
            cols = slice(at + part * HEAD, at + (part + 1) * HEAD)
            values_ref[:HEAD, cols] = msg[rows, HEAD:]
    total = len(blocks) * block
    values_ref[HEAD:, first : first + total] = jnp.ones((SUM_ROWS, total), bf16)


def blocks_of(refs):
    blocks = []
    for ref in refs:
        blocks += [ref] if len(ref.shape) == 2 else [ref.at[i] for i in range(ref.shape[0])]
    return blocks


def score(keys, queries):
    return lax.dot_general(keys, queries, (((1,), (1,)), ((), ())), preferred_element_type=f32)


def prepare_keys_kernel(keys_ref, values_ref, kind_ref, out_ref, token_ref):
    token_ref[0] = 0
    block = keys_ref.shape[0]
    out_ref[:block, :HEAD] = keys_ref[...]
    for at in range(0, block, HEAD):
        turned = values_ref[at : at + HEAD, :].astype(f32).T
        out_ref[at : at + HEAD, HEAD:] = turned.astype(bf16)
    out_ref[block:, :] = type_marks(kind_ref)


def type_marks(kind_ref):
    kinds = jnp.broadcast_to(kind_ref[...].astype(f32), (EXTRA, kind_ref.shape[1]))
    row = lax.broadcasted_iota(jnp.int32, kinds.shape, 0)
    return jnp.where(row == 0, 1.0 - kinds, jnp.where(row == 1, kinds, 0.0)).astype(bf16)


def prepare_queries_kernel(bias_ref, query_ref, kind_ref, gate_ref, out_ref, token_ref):
    token_ref[0] = 0
    marks = type_marks(kind_ref)
    row = lax.broadcasted_iota(jnp.int32, (EXTRA, HEAD), 0)
    col = lax.broadcasted_iota(jnp.int32, (EXTRA, HEAD), 1)
    for head in range(out_ref.shape[0]):
        out_ref[head, :, :HEAD] = query_ref[:, head * HEAD : (head + 1) * HEAD]
        pairs = [bias_ref[4 * head + i] * math.sqrt(HEAD) for i in range(4)]
        first = jnp.where(col % 2 == 0, pairs[0], pairs[1])
        second = jnp.where(col % 2 == 0, pairs[2], pairs[3])
        table = jnp.where(row == 0, first, jnp.where(row == 1, second, 0.0))
        high = table.astype(bf16)
        rest = table - high.astype(f32)
        middle = rest.astype(bf16)
        low = (rest - middle.astype(f32)).astype(bf16)
        group = col // 2
        terms = jnp.where(
            group == 0,
            high.astype(f32),
            jnp.where(group == 1, middle.astype(f32), jnp.where(group == 2, low.astype(f32), 0.0)),
        ).astype(bf16)
        spread = lax.dot_general(
            marks, terms, (((0,), (0,)), ((), ())), preferred_element_type=f32
        )
        out_ref[head, :, HEAD:] = spread.astype(bf16)


def own_kernel(msgs, where_ref, mine_ref, other_ref, *refs):
    state_ref, token_ref, keys_ref, values_ref = refs[msgs:]
    blocks = blocks_of(refs[:msgs])
    slots = len(blocks)
    heads, block, _ = mine_ref.shape
    lanes = 2 * block
    stage_keys(blocks, 0, keys_ref, values_ref)
    token_ref[0] = where_ref[0] * 0
    lane = lax.broadcasted_iota(jnp.int32, (block, lanes), 1)
    query_pos = jnp.where(lane < block, where_ref[0] + lane, where_ref[1] + lane - block)
    ahead = lax.broadcasted_iota(jnp.int32, (block, lanes), 0) - query_pos

    def one_head(head, carry):
        queries = jnp.concatenate([mine_ref[head], other_ref[head]], axis=0)
        at = pl.ds(pl.multiple_of(head * lanes, HEAD), lanes)
        peak = jnp.full((1, lanes), MASKED, f32)
        parts = []
        for slot in range(slots):
            piece = score(keys_ref[slot * block : (slot + 1) * block, :], queries)
            piece = jnp.where(ahead <= -where_ref[2 + slot], piece, MASKED)
            peak = jnp.maximum(peak, jnp.max(piece, axis=0, keepdims=True))
            parts.append(piece)
        peak = jnp.where(peak > 0.5 * MASKED, peak, 0.0)
        shift = peak * LOG2_SCALE
        weights = jnp.concatenate(
            [jnp.exp2(part * LOG2_SCALE - shift).astype(bf16) for part in parts], axis=0
        )
        state_ref[:ACC_ROWS, at] = jnp.dot(values_ref[...], weights, preferred_element_type=f32)
        state_ref[ACC_ROWS:, at] = jnp.broadcast_to(peak, (8, lanes))
        return carry

    lax.fori_loop(0, heads, one_head, 0)


def add_keys(
    count, mine_ref, other_ref, keys_ref, values_ref, size, old_ref, state_ref, unroll
):
    heads, block, _ = mine_ref.shape
    lanes = 2 * block
    state_ref[...] = old_ref[...]

    def queries_of(head):
        return jnp.concatenate([mine_ref[head], other_ref[head]], axis=0)

    def lanes_of(head):
        return pl.ds(pl.multiple_of(head * lanes, HEAD), lanes)

    def unit(step, worst):
        head, plane = step % heads, step // heads
        at = lanes_of(head)
        part = pl.ds(pl.multiple_of(plane * size, size), size)
        peak = old_ref[ACC_ROWS : ACC_ROWS + 1, at]
        mass = old_ref[HEAD : HEAD + 1, at]
        scores = score(keys_ref[part, :], queries_of(head))
        top = jnp.max(scores, axis=0, keepdims=True)
        weights = jnp.exp2(scores * LOG2_SCALE - peak * LOG2_SCALE).astype(bf16)
        state_ref[:ACC_ROWS, at] += jnp.dot(
            values_ref[:, part], weights, preferred_element_type=f32
        )
        rise = (top - peak) * LOG2_SCALE
        bad = (rise > ROOM) | ((mass <= 0.0) & (rise < -ROOM))
        return jnp.maximum(worst, jnp.where(bad, 1.0, 0.0))

    def units(turn, worst):
        for part in range(unroll):
            worst = unit(turn * unroll + part, worst)
        return worst

    turns = count * (heads // unroll)
    worst = lax.fori_loop(0, turns, units, jnp.zeros((1, lanes), f32))

    @pl.when(jnp.max(worst) > 0.5)
    def _():
        state_ref[...] = old_ref[...]
        step_rows = 128
        chunks = size // step_rows

        def redo(step, carry):
            at = lanes_of(step % heads)
            part = pl.ds(pl.multiple_of((step // heads) * step_rows, step_rows), step_rows)
            peak = state_ref[ACC_ROWS : ACC_ROWS + 1, at]
            mass = state_ref[HEAD : HEAD + 1, at]
            scores = score(keys_ref[part, :], queries_of(step % heads))
            top = jnp.max(scores, axis=0, keepdims=True)
            fresh = jnp.where(mass > 0.0, jnp.maximum(peak, top), top)
            fade = jnp.where(mass > 0.0, jnp.exp2((peak - fresh) * LOG2_SCALE), 0.0)
            weights = jnp.exp2(scores * LOG2_SCALE - fresh * LOG2_SCALE).astype(bf16)
            update = jnp.dot(values_ref[:, part], weights, preferred_element_type=f32)
            state_ref[:ACC_ROWS, at] = state_ref[:ACC_ROWS, at] * fade + update
            state_ref[ACC_ROWS:, at] = jnp.broadcast_to(fresh, (8, lanes))
            return carry

        lax.fori_loop(0, heads * count * chunks, redo, 0)


def plane_kernel(plan, last, gates, count_ref, mine_ref, other_ref, *refs):
    msgs = 1 + max(index for plane in plan for index, _ in plane)
    old_ref = refs[msgs]
    if last:
        kept_ref, parcel_ref, token_ref, state_ref, keys_ref, values_ref = refs[msgs + 1 + gates :]
    else:
        state_ref, token_ref, keys_ref, values_ref = refs[msgs + 1 + gates :]
    blocks = [blocks_of([ref]) for ref in refs[:msgs]]
    heads, block, _ = mine_ref.shape
    size = len(plan[0]) * block
    count = count_ref[0]
    for number, plane in enumerate(plan):

        @pl.when(count > number)
        def _(number=number, plane=plane):
            stage_keys([blocks[i][j] for i, j in plane], number * size, keys_ref, values_ref)

    unroll = 1 if last else heads
    add_keys(count, mine_ref, other_ref, keys_ref, values_ref, size, old_ref, state_ref, unroll)
    token_ref[0] = count * 0
    if not last:
        return
    for head in range(heads):
        finish(block, head, state_ref, kept_ref.at[head], parcel_ref.at[head])


def finish(block, head, state_ref, kept_ref, parcel_ref):
    at = slice(head * 2 * block, (head + 1) * 2 * block)
    mass = state_ref[HEAD : HEAD + 1, at]
    peak = state_ref[ACC_ROWS : ACC_ROWS + 1, at]
    full = mass > 0.0
    safe = jnp.where(full, mass, 1.0)
    level = jnp.where(full, peak * LOG2_SCALE + jnp.log2(safe), MASKED)
    mean = state_ref[:HEAD, at] * (1.0 / safe)
    kept_ref[:HEAD, :] = mean[:, :block]
    kept_ref[HEAD:, :] = jnp.broadcast_to(level[:, :block], (8, block))
    parcel_ref[:HEAD, :] = mean[:, block:].astype(bf16)
    whole = jnp.broadcast_to(level[:, block:], (EXTRA, block))
    high = whole.astype(bf16)
    rest = whole - high.astype(f32)
    middle = rest.astype(bf16)
    low = rest - middle.astype(f32)
    row = lax.broadcasted_iota(jnp.int32, whole.shape, 0)
    parcel_ref[HEAD:, :] = jnp.where(
        row == 0,
        high.astype(f32),
        jnp.where(row == 1, middle.astype(f32), jnp.where(row == 2, low, 0.0)),
    ).astype(bf16)


def merge_kernel(kept_ref, came_ref, low_ref, high_ref, token_ref):
    token_ref[0] = 0
    half = low_ref.shape[0]
    for head in range(kept_ref.shape[0]):
        kept_level = kept_ref[head, HEAD : HEAD + 1, :]
        extra = came_ref[head, HEAD:, :].astype(f32)
        came_level = extra[0:1] + extra[1:2] + extra[2:3]
        top = jnp.maximum(kept_level, came_level)
        kept_part = jnp.exp2(kept_level - top)
        came_part = jnp.exp2(came_level - top)
        share = 1.0 / (kept_part + came_part)
        mixed = kept_ref[head, :HEAD, :] * (kept_part * share) + came_ref[head, :HEAD, :].astype(
            f32
        ) * (came_part * share)
        cols = slice(head * HEAD, (head + 1) * HEAD)
        low_ref[:, cols] = mixed[:, :half].T.astype(bf16)
        high_ref[:, cols] = mixed[:, half:].T.astype(bf16)


def whole(value):
    return pl.BlockSpec(value.shape, lambda *_: (0,) * value.ndim)


IN_VMEM = pl.BlockSpec(memory_space=pltpu.VMEM)
IN_SMEM = pl.BlockSpec(memory_space=pltpu.SMEM)


def attend_own(where, mine, other, msgs):
    heads, block, depth = mine.shape
    lanes = 2 * block
    total = block * sum(1 if m.ndim == 2 else m.shape[0] for m in msgs)
    return pl.pallas_call(
        functools.partial(own_kernel, len(msgs)),
        in_specs=[IN_SMEM] + [IN_VMEM] * (2 + len(msgs)),
        out_specs=[IN_VMEM, IN_SMEM],
        scratch_shapes=[pltpu.VMEM((total, 2 * HEAD), bf16), pltpu.VMEM((ACC_ROWS, total), bf16)],
        out_shape=[
            jax.ShapeDtypeStruct((STATE_ROWS, heads * lanes), f32),
            jax.ShapeDtypeStruct((1,), jnp.int32),
        ],
        compiler_params=pltpu.CompilerParams(vmem_limit_bytes=VMEM_LIMIT),
        cost_estimate=pl.CostEstimate(
            flops=8 * heads * lanes * total * 256, bytes_accessed=2**20, transcendentals=0
        ),
        name="own_plane",
    )(where, mine, other, *msgs)


def attend_planes(count, mine, other, msgs, plan, state, last=False, gates=()):
    heads, block, depth = mine.shape
    lanes = 2 * block
    total = block * sum(len(plane) for plane in plan)
    scratch = [pltpu.VMEM((total, 2 * HEAD), bf16), pltpu.VMEM((ACC_ROWS, total), bf16)]
    if last:
        out_specs = [IN_VMEM, IN_VMEM, IN_SMEM]
        out_shape = [
            jax.ShapeDtypeStruct((heads, ACC_ROWS, block), f32),
            jax.ShapeDtypeStruct((heads, STATE_ROWS, block), bf16),
            jax.ShapeDtypeStruct((1,), jnp.int32),
        ]
        scratch = [pltpu.VMEM((STATE_ROWS, heads * lanes), f32)] + scratch
    else:
        out_specs = [IN_VMEM, IN_SMEM]
        out_shape = [
            jax.ShapeDtypeStruct((STATE_ROWS, heads * lanes), f32),
            jax.ShapeDtypeStruct((1,), jnp.int32),
        ]
    return pl.pallas_call(
        functools.partial(plane_kernel, plan, last, len(gates)),
        in_specs=[IN_SMEM]
        + [IN_VMEM] * (3 + len(msgs))
        + [pl.BlockSpec(memory_space=pl.ANY)] * len(gates),
        out_specs=out_specs,
        scratch_shapes=scratch,
        out_shape=out_shape,
        compiler_params=pltpu.CompilerParams(vmem_limit_bytes=VMEM_LIMIT),
        cost_estimate=pl.CostEstimate(
            flops=6 * heads * lanes * total * 256, bytes_accessed=2**20, transcendentals=0
        ),
        name="last_planes" if last else "planes",
    )(count, mine, other, *msgs, state, *gates)


def joined(pair):
    return jnp.concatenate([pair[0][...], pair[1][...]], axis=0)


def near_kernel(core_ref, own, below, above, own_w, up_w, down_w, out_ref):
    rows, width = up_w[0].shape
    out_ref[...] = jnp.dot(joined(own), own_w[...], preferred_element_type=f32)
    low, high = joined(below), joined(above)
    for side in range(2):
        first = jnp.where(core_ref[0] == side, 0, width)
        at = pl.ds(pl.multiple_of(first, HEAD), width)
        more = jnp.dot(low, up_w[side][...], preferred_element_type=f32)
        out_ref[:, at] += more + jnp.dot(high, down_w[side][...], preferred_element_type=f32)


def far_kernel(core_ref, near_ref, pair, far_w, out_ref):
    part = joined(pair)
    width = far_w[0].shape[1]
    for side in range(2):
        first = jnp.where(core_ref[0] == side, 0, width)
        at = pl.ds(pl.multiple_of(first, HEAD), width)
        more = jnp.dot(part, far_w[side][...], preferred_element_type=f32)
        out_ref[:, at] = (near_ref[:, at] + more).astype(bf16)


def project_near(core, own, below, above, own_w, up_w, down_w):
    block, cols = 2 * own[0].shape[0], own_w.shape[1]
    pair = [IN_VMEM] * 2
    return pl.pallas_call(
        near_kernel,
        in_specs=[IN_SMEM, pair, pair, pair, IN_VMEM, pair, pair],
        out_specs=IN_VMEM,
        out_shape=jax.ShapeDtypeStruct((block, cols), f32),
        compiler_params=pltpu.CompilerParams(vmem_limit_bytes=VMEM_LIMIT),
        name="project_near",
    )(core, list(own), below, above, own_w, up_w, down_w)


def project_far(core, near, opposite, far_w):
    pair = [IN_VMEM] * 2
    return pl.pallas_call(
        far_kernel,
        in_specs=[IN_SMEM, IN_VMEM, pair, pair],
        out_specs=IN_VMEM,
        out_shape=jax.ShapeDtypeStruct(near.shape, bf16),
        compiler_params=pltpu.CompilerParams(vmem_limit_bytes=VMEM_LIMIT),
        name="project_far",
    )(core, near, opposite, far_w)


def carve_kernel(column_ref, weight_ref, out_ref, sem):
    column = pl.multiple_of(column_ref[0], HEAD)
    copy = pltpu.make_async_copy(weight_ref.at[:, pl.ds(column, out_ref.shape[1])], out_ref, sem)
    copy.start()
    copy.wait()


def take_columns(column, weight, width):
    rows = weight.shape[0]
    return pl.pallas_call(
        carve_kernel,
        in_specs=[IN_SMEM, pl.BlockSpec(memory_space=pltpu.HBM)],
        out_specs=IN_VMEM,
        out_shape=jax.ShapeDtypeStruct((rows, width), weight.dtype),
        scratch_shapes=[pltpu.SemaphoreType.DMA],
        compiler_params=pltpu.CompilerParams(vmem_limit_bytes=SMALL_LIMIT),
        name="carve",
    )(column, weight)


def shift(value, axis, size, step):
    return lax.ppermute(value, axis, [(i, (i + step) % size) for i in range(size)])


def with_sibling(weight, token):
    weight = weight + token[0].astype(bf16)
    return [weight, shift(weight, "core", 2, 1)]


def shards(sizes, queries, keys, values, token_types, type_bias, out_weight):
    nz, nx, nc, ny = sizes
    zi, xi, ci, yi = (lax.axis_index(a) for a in ("z", "x", "core", "head"))
    block = queries.shape[0]
    heads = type_bias.shape[0]
    kinds = token_types.reshape(1, block)

    message, early = pl.pallas_call(
        prepare_keys_kernel,
        out_specs=[IN_VMEM, IN_SMEM],
        out_shape=[
            jax.ShapeDtypeStruct((block + EXTRA, 2 * HEAD), bf16),
            jax.ShapeDtypeStruct((1,), jnp.int32),
        ],
        name="prepare_keys",
    )(keys, values, kinds)

    across = shift(message, "x", nx, 2)
    right = shift(message, "x", nx, 1)
    left = shift(message, "x", nx, -1)
    plane = jnp.stack([message, right, across, left])
    mine, ready = pl.pallas_call(
        prepare_queries_kernel,
        in_specs=[IN_SMEM] + [IN_VMEM] * 3,
        out_specs=[IN_VMEM, IN_SMEM],
        out_shape=[
            jax.ShapeDtypeStruct((heads, block, 2 * HEAD), bf16),
            jax.ShapeDtypeStruct((1,), jnp.int32),
        ],
        name="prepare_queries",
    )(type_bias.reshape(-1), queries, kinds, plane)
    other = shift(mine, "core", nc, 1)

    forward, backward = [plane], [plane]

    def onward(token):
        zero = 0 if token is None else token[0].astype(bf16)
        forward.append(shift(forward[-1] + zero, "z", nz, 1))
        backward.append(shift(backward[-1] + zero, "z", nz, -1))

    onward(None)

    rows_w, cols_w = out_weight.shape[0], out_weight.shape[1] // ny
    half = cols_w // nc

    def column(step):
        return ((yi + step) % ny) * cols_w + ci * half

    up_w, down_w = [
        shift(
            lax.dynamic_slice(out_weight, (0, column(step) + ready[0]), (rows_w, half)),
            "head",
            ny,
            step,
        )
        for step in (1, -1)
    ]

    chip = (zi * nx + xi) * nc
    homes = [((zi * nx + (xi - d) % nx) * nc + ci) * block for d in range(nx)]
    where = jnp.stack([(chip + ci) * block, (chip + 1 - ci) * block] + homes).astype(jnp.int32)
    state, token = attend_own(where, mine, other, [plane])
    far_w = shift(
        take_columns((column(2) + token).astype(jnp.int32), out_weight, half), "head", ny, 2
    )
    onward(token)
    onward(None)
    far_parts = [forward[3][: nx // 2], backward[3][nx // 2 :]]
    far = [shift(far_parts[0], "z", nz, 1), shift(far_parts[1], "z", nz, -1)]
    planes = tuple(tuple((i, j) for j in range(nx)) for i in range(2))
    for step in (1, 2, 3):
        count = jnp.stack([jnp.where(zi >= nz - step, 2, jnp.where(zi >= step, 1, 0))])
        state, token = attend_planes(
            count.astype(jnp.int32),
            mine,
            other,
            [forward[step], backward[step]],
            planes,
            state,
            gates=far_parts if step == 3 else (),
        )
        if step == 2:
            up_w, down_w = with_sibling(up_w, token), with_sibling(down_w, token)
    count = jnp.stack([jnp.where(zi >= nz // 2, 1, 0)]).astype(jnp.int32)
    kept, parcel, token = attend_planes(
        count, mine, other, far, (((0, 0), (0, 1), (1, 0), (1, 1)),), state, last=True
    )

    came = shift(parcel, "core", nc, 1)
    *own, merged = pl.pallas_call(
        merge_kernel,
        out_specs=[IN_VMEM, IN_VMEM, IN_SMEM],
        out_shape=[jax.ShapeDtypeStruct((block // 2, heads * HEAD), bf16)] * 2
        + [jax.ShapeDtypeStruct((1,), jnp.int32)],
        compiler_params=pltpu.CompilerParams(vmem_limit_bytes=SMALL_LIMIT),
        name="merge",
    )(kept, came)

    below = [shift(own[0], "head", ny, 1), None]
    above = [None, shift(own[1], "head", ny, -1)]
    below[1] = shift(own[1], "head", ny, 1)
    above[0] = shift(own[0], "head", ny, -1)
    opposite = [shift(below[0], "head", ny, 1), shift(above[1], "head", ny, -1)]
    own_w = lax.dynamic_slice(out_weight, (0, yi * cols_w + token[0]), (rows_w, cols_w))
    core = jnp.stack([ci]).astype(jnp.int32)
    near = project_near(core, own, below, above, own_w, up_w, down_w)
    return project_far(core, near, opposite, with_sibling(far_w, merged))


def solution(mesh):
    nz, nx, nc, ny = 8, 4, 2, 4
    grid = Mesh(mesh.devices.reshape(nz, nx, nc, ny), ("z", "x", "core", "head"))
    ctx = ("z", "x", "core")
    in_specs = (
        P(ctx, "head"),
        P(ctx, "head"),
        P(ctx, "head"),
        P(ctx),
        P("head", None, None),
        P("head", None),
    )
    return jax.shard_map(
        functools.partial(shards, (nz, nx, nc, ny)),
        mesh=grid,
        in_specs=in_specs,
        out_specs=P(ctx, "head"),
        check_vma=False,
    )
```

```python
import functools
import math

import jax
import jax.numpy as jnp
from jax import lax
from jax.experimental import pallas as pl
from jax.experimental.pallas import tpu as pltpu
from jax.sharding import Mesh, PartitionSpec as P

f32 = jnp.float32
bf16 = jnp.bfloat16
HEAD = 128
EXTRA = 16
SUM_ROWS = 8
ACC_ROWS = HEAD + SUM_ROWS
STATE_ROWS = ACC_ROWS + 8
MASKED = -1e30
ROOM = 64.0
VMEM_LIMIT = 12 * 2**20
SMALL_LIMIT = 8 * 2**20
LOG2_SCALE = 1.4426950408889634 / math.sqrt(HEAD)


def stage_keys(blocks, first, keys_ref, values_ref):
    block = blocks[0].shape[0] - EXTRA
    row = lax.broadcasted_iota(jnp.int32, (EXTRA, HEAD), 0)
    col = lax.broadcasted_iota(jnp.int32, (EXTRA, HEAD), 1)
    spread = jnp.where((row < 2) & (col < 6) & (col % 2 == row), 1.0, 0.0).astype(bf16)
    for number, msg in enumerate(blocks):
        at = first + number * block
        keys_ref[at : at + block, :HEAD] = msg[:block, :HEAD]
        marks = lax.dot_general(
            msg[block:, :], spread, (((0,), (0,)), ((), ())), preferred_element_type=f32
        )
        keys_ref[at : at + block, HEAD:] = marks.astype(bf16)
        for part in range(block // HEAD):
            rows = slice(part * HEAD, (part + 1) * HEAD)
            cols = slice(at + part * HEAD, at + (part + 1) * HEAD)
            values_ref[:HEAD, cols] = msg[rows, HEAD:]
    total = len(blocks) * block
    values_ref[HEAD:, first : first + total] = jnp.ones((SUM_ROWS, total), bf16)


def blocks_of(refs):
    blocks = []
    for ref in refs:
        blocks += [ref] if len(ref.shape) == 2 else [ref.at[i] for i in range(ref.shape[0])]
    return blocks


def score(keys, queries):
    return lax.dot_general(keys, queries, (((1,), (1,)), ((), ())), preferred_element_type=f32)


def prepare_keys_kernel(keys_ref, values_ref, kind_ref, out_ref, token_ref):
    token_ref[0] = 0
    block = keys_ref.shape[0]
    out_ref[:block, :HEAD] = keys_ref[...]
    for at in range(0, block, HEAD):
        turned = values_ref[at : at + HEAD, :].astype(f32).T
        out_ref[at : at + HEAD, HEAD:] = turned.astype(bf16)
    out_ref[block:, :] = type_marks(kind_ref)


def type_marks(kind_ref):
    kinds = jnp.broadcast_to(kind_ref[...].astype(f32), (EXTRA, kind_ref.shape[1]))
    row = lax.broadcasted_iota(jnp.int32, kinds.shape, 0)
    return jnp.where(row == 0, 1.0 - kinds, jnp.where(row == 1, kinds, 0.0)).astype(bf16)


def prepare_queries_kernel(bias_ref, query_ref, kind_ref, gate_ref, out_ref, token_ref):
    token_ref[0] = 0
    marks = type_marks(kind_ref)
    row = lax.broadcasted_iota(jnp.int32, (EXTRA, HEAD), 0)
    col = lax.broadcasted_iota(jnp.int32, (EXTRA, HEAD), 1)
    for head in range(out_ref.shape[0]):
        out_ref[head, :, :HEAD] = query_ref[:, head * HEAD : (head + 1) * HEAD]
        pairs = [bias_ref[4 * head + i] * math.sqrt(HEAD) for i in range(4)]
        first = jnp.where(col % 2 == 0, pairs[0], pairs[1])
        second = jnp.where(col % 2 == 0, pairs[2], pairs[3])
        table = jnp.where(row == 0, first, jnp.where(row == 1, second, 0.0))
        high = table.astype(bf16)
        rest = table - high.astype(f32)
        middle = rest.astype(bf16)
        low = (rest - middle.astype(f32)).astype(bf16)
        group = col // 2
        terms = jnp.where(
            group == 0,
            high.astype(f32),
            jnp.where(group == 1, middle.astype(f32), jnp.where(group == 2, low.astype(f32), 0.0)),
        ).astype(bf16)
        spread = lax.dot_general(
            marks, terms, (((0,), (0,)), ((), ())), preferred_element_type=f32
        )
        out_ref[head, :, HEAD:] = spread.astype(bf16)


def own_kernel(msgs, where_ref, mine_ref, other_ref, *refs):
    state_ref, token_ref, keys_ref, values_ref = refs[msgs:]
    blocks = blocks_of(refs[:msgs])
    slots = len(blocks)
    heads, block, _ = mine_ref.shape
    lanes = 2 * block
    stage_keys(blocks, 0, keys_ref, values_ref)
    token_ref[0] = where_ref[0] * 0
    lane = lax.broadcasted_iota(jnp.int32, (block, lanes), 1)
    query_pos = jnp.where(lane < block, where_ref[0] + lane, where_ref[1] + lane - block)
    ahead = lax.broadcasted_iota(jnp.int32, (block, lanes), 0) - query_pos

    def one_head(head, carry):
        queries = jnp.concatenate([mine_ref[head], other_ref[head]], axis=0)
        at = pl.ds(pl.multiple_of(head * lanes, HEAD), lanes)
        peak = jnp.full((1, lanes), MASKED, f32)
        parts = []
        for slot in range(slots):
            piece = score(keys_ref[slot * block : (slot + 1) * block, :], queries)
            piece = jnp.where(ahead <= -where_ref[2 + slot], piece, MASKED)
            peak = jnp.maximum(peak, jnp.max(piece, axis=0, keepdims=True))
            parts.append(piece)
        peak = jnp.where(peak > 0.5 * MASKED, peak, 0.0)
        shift = peak * LOG2_SCALE
        weights = jnp.concatenate(
            [jnp.exp2(part * LOG2_SCALE - shift).astype(bf16) for part in parts], axis=0
        )
        state_ref[:ACC_ROWS, at] = jnp.dot(values_ref[...], weights, preferred_element_type=f32)
        state_ref[ACC_ROWS:, at] = jnp.broadcast_to(peak, (8, lanes))
        return carry

    lax.fori_loop(0, heads, one_head, 0)


def add_keys(
    count, mine_ref, other_ref, keys_ref, values_ref, size, old_ref, state_ref, unroll
):
    heads, block, _ = mine_ref.shape
    lanes = 2 * block
    state_ref[...] = old_ref[...]

    def queries_of(head):
        return jnp.concatenate([mine_ref[head], other_ref[head]], axis=0)

    def lanes_of(head):
        return pl.ds(pl.multiple_of(head * lanes, HEAD), lanes)

    def unit(step, worst):
        head, plane = step % heads, step // heads
        at = lanes_of(head)
        part = pl.ds(pl.multiple_of(plane * size, size), size)
        peak = old_ref[ACC_ROWS : ACC_ROWS + 1, at]
        mass = old_ref[HEAD : HEAD + 1, at]
        scores = score(keys_ref[part, :], queries_of(head))
        top = jnp.max(scores, axis=0, keepdims=True)
        weights = jnp.exp2(scores * LOG2_SCALE - peak * LOG2_SCALE).astype(bf16)
        state_ref[:ACC_ROWS, at] += jnp.dot(
            values_ref[:, part], weights, preferred_element_type=f32
        )
        rise = (top - peak) * LOG2_SCALE
        bad = (rise > ROOM) | ((mass <= 0.0) & (rise < -ROOM))
        return jnp.maximum(worst, jnp.where(bad, 1.0, 0.0))

    def units(turn, worst):
        for part in range(unroll):
            worst = unit(turn * unroll + part, worst)
        return worst

    turns = count * (heads // unroll)
    worst = lax.fori_loop(0, turns, units, jnp.zeros((1, lanes), f32))

    @pl.when(jnp.max(worst) > 0.5)
    def _():
        state_ref[...] = old_ref[...]
        step_rows = 128
        chunks = size // step_rows

        def redo(step, carry):
            at = lanes_of(step % heads)
            part = pl.ds(pl.multiple_of((step // heads) * step_rows, step_rows), step_rows)
            peak = state_ref[ACC_ROWS : ACC_ROWS + 1, at]
            mass = state_ref[HEAD : HEAD + 1, at]
            scores = score(keys_ref[part, :], queries_of(step % heads))
            top = jnp.max(scores, axis=0, keepdims=True)
            fresh = jnp.where(mass > 0.0, jnp.maximum(peak, top), top)
            fade = jnp.where(mass > 0.0, jnp.exp2((peak - fresh) * LOG2_SCALE), 0.0)
            weights = jnp.exp2(scores * LOG2_SCALE - fresh * LOG2_SCALE).astype(bf16)
            update = jnp.dot(values_ref[:, part], weights, preferred_element_type=f32)
            state_ref[:ACC_ROWS, at] = state_ref[:ACC_ROWS, at] * fade + update
            state_ref[ACC_ROWS:, at] = jnp.broadcast_to(fresh, (8, lanes))
            return carry

        lax.fori_loop(0, heads * count * chunks, redo, 0)


def plane_kernel(plan, last, gates, count_ref, mine_ref, other_ref, *refs):
    msgs = 1 + max(index for plane in plan for index, _ in plane)
    old_ref = refs[msgs]
    if last:
        kept_ref, parcel_ref, token_ref, state_ref, keys_ref, values_ref = refs[msgs + 1 + gates :]
    else:
        state_ref, token_ref, keys_ref, values_ref = refs[msgs + 1 + gates :]
    blocks = [blocks_of([ref]) for ref in refs[:msgs]]
    heads, block, _ = mine_ref.shape
    size = len(plan[0]) * block
    count = count_ref[0]
    for number, plane in enumerate(plan):

        @pl.when(count > number)
        def _(number=number, plane=plane):
            stage_keys([blocks[i][j] for i, j in plane], number * size, keys_ref, values_ref)

    unroll = 1 if last else heads
    add_keys(count, mine_ref, other_ref, keys_ref, values_ref, size, old_ref, state_ref, unroll)
    token_ref[0] = count * 0
    if not last:
        return
    for head in range(heads):
        finish(block, head, state_ref, kept_ref.at[head], parcel_ref.at[head])


def finish(block, head, state_ref, kept_ref, parcel_ref):
    at = slice(head * 2 * block, (head + 1) * 2 * block)
    mass = state_ref[HEAD : HEAD + 1, at]
    peak = state_ref[ACC_ROWS : ACC_ROWS + 1, at]
    full = mass > 0.0
    safe = jnp.where(full, mass, 1.0)
    level = jnp.where(full, peak * LOG2_SCALE + jnp.log2(safe), MASKED)
    mean = state_ref[:HEAD, at] * (1.0 / safe)
    kept_ref[:HEAD, :] = mean[:, :block]
    kept_ref[HEAD:, :] = jnp.broadcast_to(level[:, :block], (8, block))
    parcel_ref[:HEAD, :] = mean[:, block:].astype(bf16)
    whole = jnp.broadcast_to(level[:, block:], (EXTRA, block))
    high = whole.astype(bf16)
    rest = whole - high.astype(f32)
    middle = rest.astype(bf16)
    low = rest - middle.astype(f32)
    row = lax.broadcasted_iota(jnp.int32, whole.shape, 0)
    parcel_ref[HEAD:, :] = jnp.where(
        row == 0,
        high.astype(f32),
        jnp.where(row == 1, middle.astype(f32), jnp.where(row == 2, low, 0.0)),
    ).astype(bf16)


def merge_kernel(kept_ref, came_ref, low_ref, high_ref, token_ref):
    token_ref[0] = 0
    half = low_ref.shape[0]
    for head in range(kept_ref.shape[0]):
        kept_level = kept_ref[head, HEAD : HEAD + 1, :]
        extra = came_ref[head, HEAD:, :].astype(f32)
        came_level = extra[0:1] + extra[1:2] + extra[2:3]
        top = jnp.maximum(kept_level, came_level)
        kept_part = jnp.exp2(kept_level - top)
        came_part = jnp.exp2(came_level - top)
        share = 1.0 / (kept_part + came_part)
        mixed = kept_ref[head, :HEAD, :] * (kept_part * share) + came_ref[head, :HEAD, :].astype(
            f32
        ) * (came_part * share)
        cols = slice(head * HEAD, (head + 1) * HEAD)
        low_ref[:, cols] = mixed[:, :half].T.astype(bf16)
        high_ref[:, cols] = mixed[:, half:].T.astype(bf16)


def whole(value):
    return pl.BlockSpec(value.shape, lambda *_: (0,) * value.ndim)


IN_VMEM = pl.BlockSpec(memory_space=pltpu.VMEM)
IN_SMEM = pl.BlockSpec(memory_space=pltpu.SMEM)


def attend_own(where, mine, other, msgs):
    heads, block, depth = mine.shape
    lanes = 2 * block
    total = block * sum(1 if m.ndim == 2 else m.shape[0] for m in msgs)
    return pl.pallas_call(
        functools.partial(own_kernel, len(msgs)),
        in_specs=[IN_SMEM] + [IN_VMEM] * (2 + len(msgs)),
        out_specs=[IN_VMEM, IN_SMEM],
        scratch_shapes=[pltpu.VMEM((total, 2 * HEAD), bf16), pltpu.VMEM((ACC_ROWS, total), bf16)],
        out_shape=[
            jax.ShapeDtypeStruct((STATE_ROWS, heads * lanes), f32),
            jax.ShapeDtypeStruct((1,), jnp.int32),
        ],
        compiler_params=pltpu.CompilerParams(vmem_limit_bytes=VMEM_LIMIT),
        cost_estimate=pl.CostEstimate(
            flops=8 * heads * lanes * total * 256, bytes_accessed=2**20, transcendentals=0
        ),
        name="own_plane",
    )(where, mine, other, *msgs)


def attend_planes(count, mine, other, msgs, plan, state, last=False, gates=()):
    heads, block, depth = mine.shape
    lanes = 2 * block
    total = block * sum(len(plane) for plane in plan)
    scratch = [pltpu.VMEM((total, 2 * HEAD), bf16), pltpu.VMEM((ACC_ROWS, total), bf16)]
    if last:
        out_specs = [IN_VMEM, IN_VMEM, IN_SMEM]
        out_shape = [
            jax.ShapeDtypeStruct((heads, ACC_ROWS, block), f32),
            jax.ShapeDtypeStruct((heads, STATE_ROWS, block), bf16),
            jax.ShapeDtypeStruct((1,), jnp.int32),
        ]
        scratch = [pltpu.VMEM((STATE_ROWS, heads * lanes), f32)] + scratch
    else:
        out_specs = [IN_VMEM, IN_SMEM]
        out_shape = [
            jax.ShapeDtypeStruct((STATE_ROWS, heads * lanes), f32),
            jax.ShapeDtypeStruct((1,), jnp.int32),
        ]
    return pl.pallas_call(
        functools.partial(plane_kernel, plan, last, len(gates)),
        in_specs=[IN_SMEM]
        + [IN_VMEM] * (3 + len(msgs))
        + [pl.BlockSpec(memory_space=pl.ANY)] * len(gates),
        out_specs=out_specs,
        scratch_shapes=scratch,
        out_shape=out_shape,
        compiler_params=pltpu.CompilerParams(vmem_limit_bytes=VMEM_LIMIT),
        cost_estimate=pl.CostEstimate(
            flops=6 * heads * lanes * total * 256, bytes_accessed=2**20, transcendentals=0
        ),
        name="last_planes" if last else "planes",
    )(count, mine, other, *msgs, state, *gates)


def joined(pair):
    return jnp.concatenate([pair[0][...], pair[1][...]], axis=0)


def near_kernel(core_ref, own, below, above, own_w, up_w, down_w, out_ref):
    rows, width = up_w[0].shape
    out_ref[...] = jnp.dot(joined(own), own_w[...], preferred_element_type=f32)
    low, high = joined(below), joined(above)
    for side in range(2):
        first = jnp.where(core_ref[0] == side, 0, width)
        at = pl.ds(pl.multiple_of(first, HEAD), width)
        more = jnp.dot(low, up_w[side][...], preferred_element_type=f32)
        out_ref[:, at] += more + jnp.dot(high, down_w[side][...], preferred_element_type=f32)


def far_kernel(core_ref, near_ref, pair, far_w, out_ref):
    part = joined(pair)
    width = far_w[0].shape[1]
    for side in range(2):
        first = jnp.where(core_ref[0] == side, 0, width)
        at = pl.ds(pl.multiple_of(first, HEAD), width)
        more = jnp.dot(part, far_w[side][...], preferred_element_type=f32)
        out_ref[:, at] = (near_ref[:, at] + more).astype(bf16)


def project_near(core, own, below, above, own_w, up_w, down_w):
    block, cols = 2 * own[0].shape[0], own_w.shape[1]
    pair = [IN_VMEM] * 2
    return pl.pallas_call(
        near_kernel,
        in_specs=[IN_SMEM, pair, pair, pair, IN_VMEM, pair, pair],
        out_specs=IN_VMEM,
        out_shape=jax.ShapeDtypeStruct((block, cols), f32),
        compiler_params=pltpu.CompilerParams(vmem_limit_bytes=VMEM_LIMIT),
        name="project_near",
    )(core, list(own), below, above, own_w, up_w, down_w)


def project_far(core, near, opposite, far_w):
    pair = [IN_VMEM] * 2
    return pl.pallas_call(
        far_kernel,
        in_specs=[IN_SMEM, IN_VMEM, pair, pair],
        out_specs=IN_VMEM,
        out_shape=jax.ShapeDtypeStruct(near.shape, bf16),
        compiler_params=pltpu.CompilerParams(vmem_limit_bytes=VMEM_LIMIT),
        name="project_far",
    )(core, near, opposite, far_w)


def carve_kernel(column_ref, weight_ref, out_ref, sem):
    column = pl.multiple_of(column_ref[0], HEAD)
    copy = pltpu.make_async_copy(weight_ref.at[:, pl.ds(column, out_ref.shape[1])], out_ref, sem)
    copy.start()
    copy.wait()


def take_columns(column, weight, width):
    rows = weight.shape[0]
    return pl.pallas_call(
        carve_kernel,
        in_specs=[IN_SMEM, pl.BlockSpec(memory_space=pltpu.HBM)],
        out_specs=IN_VMEM,
        out_shape=jax.ShapeDtypeStruct((rows, width), weight.dtype),
        scratch_shapes=[pltpu.SemaphoreType.DMA],
        compiler_params=pltpu.CompilerParams(vmem_limit_bytes=SMALL_LIMIT),
        name="carve",
    )(column, weight)


def shift(value, axis, size, step):
    return lax.ppermute(value, axis, [(i, (i + step) % size) for i in range(size)])


def with_sibling(weight, token):
    weight = weight + token[0].astype(bf16)
    return [weight, shift(weight, "core", 2, 1)]


def shards(sizes, queries, keys, values, token_types, type_bias, out_weight):
    nz, nx, nc, ny = sizes
    zi, xi, ci, yi = (lax.axis_index(a) for a in ("z", "x", "core", "head"))
    block = queries.shape[0]
    heads = type_bias.shape[0]
    kinds = token_types.reshape(1, block)

    message, early = pl.pallas_call(
        prepare_keys_kernel,
        out_specs=[IN_VMEM, IN_SMEM],
        out_shape=[
            jax.ShapeDtypeStruct((block + EXTRA, 2 * HEAD), bf16),
            jax.ShapeDtypeStruct((1,), jnp.int32),
        ],
        name="prepare_keys",
    )(keys, values, kinds)

    across = shift(message, "x", nx, 2)
    right = shift(message, "x", nx, 1)
    left = shift(message, "x", nx, -1)
    plane = jnp.stack([message, right, across, left])
    mine, ready = pl.pallas_call(
        prepare_queries_kernel,
        in_specs=[IN_SMEM] + [IN_VMEM] * 3,
        out_specs=[IN_VMEM, IN_SMEM],
        out_shape=[
            jax.ShapeDtypeStruct((heads, block, 2 * HEAD), bf16),
            jax.ShapeDtypeStruct((1,), jnp.int32),
        ],
        name="prepare_queries",
    )(type_bias.reshape(-1), queries, kinds, plane)
    other = shift(mine, "core", nc, 1)

    forward, backward = [plane], [plane]

    def up(step):
        return [(i, i + 1) for i in range(step - 1, nz - 1)]

    def down(step):
        return [((q - step + 1) % nz, (q - step) % nz) for q in range(nz // 2)]

    def onward(token):
        zero = 0 if token is None else token[0].astype(bf16)
        step = len(forward)
        forward.append(lax.ppermute(forward[-1] + zero, "z", up(step)))
        backward.append(lax.ppermute(backward[-1] + zero, "z", down(step)))

    onward(None)

    rows_w, cols_w = out_weight.shape[0], out_weight.shape[1] // ny
    half = cols_w // nc

    def column(step):
        return ((yi + step) % ny) * cols_w + ci * half

    up_w, down_w = [
        shift(
            lax.dynamic_slice(out_weight, (0, column(step) + ready[0]), (rows_w, half)),
            "head",
            ny,
            step,
        )
        for step in (1, -1)
    ]

    chip = (zi * nx + xi) * nc
    homes = [((zi * nx + (xi - d) % nx) * nc + ci) * block for d in range(nx)]
    where = jnp.stack([(chip + ci) * block, (chip + 1 - ci) * block] + homes).astype(jnp.int32)
    state, token = attend_own(where, mine, other, [plane])
    far_w = shift(
        take_columns((column(2) + token).astype(jnp.int32), out_weight, half), "head", ny, 2
    )
    onward(token)
    onward(None)
    far_parts = [forward[3][: nx // 2], backward[3][nx // 2 :]]
    far = [
        lax.ppermute(far_parts[0], "z", up(nz // 2)),
        lax.ppermute(far_parts[1], "z", down(nz // 2)),
    ]
    planes = tuple(tuple((i, j) for j in range(nx)) for i in range(2))
    for step in (1, 2, 3):
        count = jnp.stack([jnp.where(zi >= nz - step, 2, jnp.where(zi >= step, 1, 0))])
        state, token = attend_planes(
            count.astype(jnp.int32),
            mine,
            other,
            [forward[step], backward[step]],
            planes,
            state,
            gates=far_parts if step == 3 else (),
        )
        if step == 2:
            up_w, down_w = with_sibling(up_w, token), with_sibling(down_w, token)
    count = jnp.stack([jnp.where(zi >= nz // 2, 1, 0)]).astype(jnp.int32)
    kept, parcel, token = attend_planes(
        count, mine, other, far, (((0, 0), (0, 1), (1, 0), (1, 1)),), state, last=True
    )

    came = shift(parcel, "core", nc, 1)
    *own, merged = pl.pallas_call(
        merge_kernel,
        out_specs=[IN_VMEM, IN_VMEM, IN_SMEM],
        out_shape=[jax.ShapeDtypeStruct((block // 2, heads * HEAD), bf16)] * 2
        + [jax.ShapeDtypeStruct((1,), jnp.int32)],
        compiler_params=pltpu.CompilerParams(vmem_limit_bytes=SMALL_LIMIT),
        name="merge",
    )(kept, came)

    below = [shift(own[0], "head", ny, 1), None]
    above = [None, shift(own[1], "head", ny, -1)]
    below[1] = shift(own[1], "head", ny, 1)
    above[0] = shift(own[0], "head", ny, -1)
    opposite = [shift(below[0], "head", ny, 1), shift(above[1], "head", ny, -1)]
    own_w = lax.dynamic_slice(out_weight, (0, yi * cols_w + token[0]), (rows_w, cols_w))
    core = jnp.stack([ci]).astype(jnp.int32)
    near = project_near(core, own, below, above, own_w, up_w, down_w)
    return project_far(core, near, opposite, with_sibling(far_w, merged))


def solution(mesh):
    nz, nx, nc, ny = 8, 4, 2, 4
    grid = Mesh(mesh.devices.reshape(nz, nx, nc, ny), ("z", "x", "core", "head"))
    ctx = ("z", "x", "core")
    in_specs = (
        P(ctx, "head"),
        P(ctx, "head"),
        P(ctx, "head"),
        P(ctx),
        P("head", None, None),
        P("head", None),
    )
    return jax.shard_map(
        functools.partial(shards, (nz, nx, nc, ny)),
        mesh=grid,
        in_specs=in_specs,
        out_specs=P(ctx, "head"),
        check_vma=False,
    )
```
